128 devices in a mesh: gx: 8 (over y, core), gy: 16 (over z, x).
Axes of the slice: x: 4, y: 4, z: 4, core: 2. Of those that a mesh axis runs over, the one named last changes fastest.
Arguments:
- q_now: float32 [5, 128, 256, 256], P(None, 'gx', 'gy'), may hold values from -6 to 6
- q_prev: float32 [5, 128, 256, 256], P(None, 'gx', 'gy'), may hold values from -6 to 6
- jacobian: float32 [128, 256, 256], P('gx', 'gy'), may hold values from 0.5 to 2
- flux_split: float32 [3, 2, 5, 5], replicated, may hold values from -2 to 2
- donor_base: int32 [131072], P(('gx', 'gy')), may hold values from 0 to 57374
- donor_frac: float32 [3, 131072], P(None, ('gx', 'gy')), may hold values from 0 to 1
- fringe_dest: int32 [131072, 1], P(('gx', 'gy')), may hold values from 0 to 127; in each aligned block of 1024 rows (0 to 1023, 1024 to 2047, ...) at most 16 rows name the same one
- receptor_cell: int32 [131072], P(('gx', 'gy')), may hold values from 0 to 65535
- fringe_count: int32 [128], P(('gx', 'gy')), may hold values from 1 to 1024, 98304 in all
Outputs:
- q_next: float32 [5, 128, 256, 256], P(None, 'gx', 'gy')
The draws below stay inside these ranges and needn't reach their ends.
Inputs may be any that keep to these rules, and one draw needn't show every extreme that they name: `fringe_dest`: among the 1024 rows of one block, at most 16 name the same destination block; some block sends exactly 16 to one destination. A block's live rows are its first fringe_count rows; the counts sum to 98304 and some block has 1024. `receptor_cell`: several rows may share a receptor cell.
All inputs are finite; a program needn't handle non-finite values.
Results may differ from the reference program's by a relative error of at most 0.0003.
Values sent between devices are 32-bit elements; how exact they have to be, the bound alone decides.
A program may use at most 192 MiB of HBM per device.

```python
import math
import jax
import jax.numpy as jnp
import numpy as np
from jax import lax

VARS = 5
CX = 16
CY = 16
CZ = 256
F_DEV = 1024
SUBITERS = 2
CELLS = 65536
CAP = 16
ROWS = 131072
NX = 128
NY = 256
N_GX = 8
N_GY = 16
DEVICES = 128


def place_ends(entries, stream_key, smallest, high):
    index_at = [jax.random.randint(jax.random.fold_in(stream_key, axis), (), 0, length) for axis, length in enumerate(entries.shape)]
    widest = entries.shape.index(max(entries.shape))
    beside = index_at[:widest] + [(index_at[widest] + 1) % entries.shape[widest]] + index_at[widest + 1:]
    return entries.at[tuple(index_at)].set(smallest).at[tuple(beside)].set(high)


def level_of(rng, shape, cuts, low, high):
    level = 1.0
    for dim, blocks in cuts:
        draws = jax.random.uniform(jax.random.fold_in(jax.random.fold_in(rng, 6), dim), (blocks,), jnp.float32, low / len(cuts), high / len(cuts))
        level = level * jnp.repeat(jnp.exp(draws), shape[dim] // blocks).reshape((-1,) + (1,) * (len(shape) - 1 - dim))
    return level


def length_profile(amount, total, bound, lean):
    weights = [(1 << 20) // math.isqrt(grade ** lean) + 1 for grade in range(2, amount + 1)]
    rest, holding = total - bound - (amount - 1), [1] * (amount - 1)
    while rest > 0:
        movable = [i for i in range(amount - 1) if holding[i] < bound]
        pool, remaining = sum([weights[i] for i in movable]), rest
        for i in movable:
            extra = min(bound - holding[i], max(1, remaining * weights[i] // pool), rest)
            holding[i] = holding[i] + extra
            rest = rest - extra
    return np.array([bound] + holding)


def uneven(stream_key, count, total, reach, slope):
    if count == 2:
        one = jax.random.randint(stream_key, (), max(1, total - reach), min(reach, total - 1) + 1)
        return jnp.stack([one, total - one])
    lengths = jnp.asarray(length_profile(count, total, reach, slope), jnp.int32)
    twos = (count - 1) // 2
    donor, sink = lengths[1:1 + 2 * twos:2], lengths[2:2 + 2 * twos:2]
    margin = jnp.minimum(donor - 1, reach - sink)
    passed = jax.random.randint(jax.random.fold_in(stream_key, 1), (twos,), 0, 1 << 20) % (margin + 1)
    lengths = lengths.at[1:1 + 2 * twos:2].set(donor - passed).at[2:2 + 2 * twos:2].set(sink + passed)
    return lengths[jax.random.permutation(jax.random.fold_in(stream_key, 2), count)]


def shared_out(key, own, number, rows, count, top, most, lean):
    order = jax.random.permutation(key, count)
    heavy_load, usual = portions_of(count, rows * top, most, lean, True), portions_of(count, rows * top, most, lean, False)
    places = jnp.arange(count)

    def named(sizes, offset_by):
        used = int((sizes > 0).sum())
        fixed = max(1, used // 4)
        passed = fixed + (places - fixed + offset_by * (used - fixed)) % max(1, count - fixed)
        return jnp.zeros((count,), jnp.int32).at[order[jnp.where(places < fixed, places, passed)]].set(jnp.asarray(sizes, jnp.int32))

    sizes = jnp.where(number % 4 == 0, named(heavy_load, number // 4), named(usual, number - number // 4 - 1))
    mixed = jax.random.permutation(jax.random.fold_in(own, 3), count)
    source_of, receiver = mixed[0:count // 2 * 2:2], mixed[1:count // 2 * 2:2]
    room = jnp.minimum(sizes[source_of] - 1, most - sizes[receiver]) // 2
    room = jnp.where((source_of == order[0]) | (receiver == order[0]) | (sizes[receiver] == 0), 0, jnp.maximum(room, 0))
    passed = jax.random.randint(jax.random.fold_in(own, 4), (count // 2,), 0, 1 << 20) % (room + 1)
    sizes = sizes.at[source_of].add(-passed).at[receiver].add(passed)
    members = jnp.searchsorted(jnp.cumsum(sizes), jnp.arange(rows * top), side="right").astype(jnp.int32)
    table = members.reshape(top, rows).T
    table = table[jax.random.permutation(jax.random.fold_in(own, 1), rows)]
    offset_by = jax.random.randint(jax.random.fold_in(own, 2), (rows, 1), 0, top)
    return jnp.take_along_axis(table, (jnp.arange(top)[None, :] + offset_by) % top, axis=1)


def portions_of(amount, total, limit, skew, full):
    loads = [(1 << 20) // math.isqrt(rank ** skew) + 1 for rank in range(1, amount + 1)]
    largest = limit if full else min(limit, max(-(-total // amount), total * loads[0] // sum(loads)))
    least = 1 if total - largest >= amount - 1 else 0
    counts, rest = [largest] + [least] * (amount - 1), total - largest - least * (amount - 1)
    while rest > 0:
        free = [i for i in range(1, amount) if counts[i] < largest] or [i for i in range(1, amount) if counts[i] < limit]
        whole, budget = sum([loads[i] for i in free]), rest
        for i in free:
            extra = min(limit - counts[i], max(1, budget * loads[i] // whole), rest)
            counts[i] = counts[i] + extra
            rest = rest - extra
    return np.array(counts)


def gaussian(rng, dims, deviation, limit, split=(), held_as=jnp.bfloat16):
    entries = deviation * jax.random.normal(rng, dims, jnp.float32)
    if split:
        entries = entries * level_of(rng, dims, split, -0.22, 0.18)
    return jnp.clip(entries, -limit, limit).astype(held_as)


def setup_inputs(seed: int = 0) -> dict:
    seeds = jax.random.split(jax.random.key(seed), 10)
    q_now = gaussian(seeds[0], (VARS, NX, NY, CZ), 1.0, 6.0, ((1, 8), (2, 16)), jnp.float32)
    q_prev = gaussian(seeds[1], (VARS, NX, NY, CZ), 1.0, 6.0, ((1, 8), (2, 16)), jnp.float32)
    jacobian = jnp.clip(jnp.exp(math.log(2.0) - 1.3862944 * jax.random.uniform(seeds[2], (NX, NY, CZ), jnp.float32) ** level_of(seeds[2], (NX, NY, CZ), ((0, 8), (1, 16)), -0.2, 0.2)), 0.5, 2.0)
    flux_split = gaussian(seeds[3], (3, 2, VARS, VARS), 10 ** -0.5, 2.0, (), jnp.float32)
    donor_base = place_ends(jax.random.randint(seeds[4], (ROWS,), 0, (CX - 1) * (CY - 1) * (CZ - 1)), jax.random.fold_in(seeds[4], 1), 0, ((CX - 1) * (CY - 1) * (CZ - 1)) - 1).astype(jnp.int32)
    donor_frac = jnp.clip(1.0 * jax.random.uniform(seeds[5], (3, ROWS), jnp.float32) ** level_of(seeds[5], (3, ROWS), ((1, 128),), -0.2, 0.2), 0.0, 1.0)
    fringe_dest_keys = jax.random.split(jax.random.fold_in(seeds[6], 1), ROWS // F_DEV)
    fringe_dest_turns = jax.random.permutation(jax.random.fold_in(seeds[6], 3), ROWS // F_DEV)
    fringe_dest = jax.vmap(lambda own, number: shared_out(jax.random.fold_in(seeds[6], 2), own, number, F_DEV, DEVICES, 1, CAP, 2))(fringe_dest_keys, fringe_dest_turns).reshape((ROWS, 1))
    receptor_cell = place_ends(jax.random.randint(seeds[7], (ROWS,), 0, CELLS), jax.random.fold_in(seeds[7], 1), 0, CELLS - 1).astype(jnp.int32)
    fringe_count = uneven(seeds[8], DEVICES, DEVICES * F_DEV * 3 // 4, F_DEV, 2).astype(jnp.int32)
    return {"q_now": q_now, "q_prev": q_prev, "jacobian": jacobian, "flux_split": flux_split, "donor_base": donor_base, "donor_frac": donor_frac, "fringe_dest": fringe_dest, "receptor_cell": receptor_cell, "fringe_count": fringe_count}


step_tau = 0.2
step_phys = 0.5
penalty = 2.0


def mixing(matrix, field):
    return jnp.einsum("ab,bxyz->axyz", matrix, field, precision=lax.Precision.HIGHEST)


def residual_padded(padded, flux_split):
    centre = padded[:, 1:-1, 1:-1, 1:-1]
    behind = [padded[:, :-2, 1:-1, 1:-1], padded[:, 1:-1, :-2, 1:-1], padded[:, 1:-1, 1:-1, :-2]]
    ahead = [padded[:, 2:, 1:-1, 1:-1], padded[:, 1:-1, 2:, 1:-1], padded[:, 1:-1, 1:-1, 2:]]
    total = jnp.zeros(centre.shape, jnp.float32)
    for direction in range(3):
        total = total + mixing(flux_split[direction, 0], centre - behind[direction])
        total = total + mixing(flux_split[direction, 1], ahead[direction] - centre)
    return total


def to_blocks(field):
    shaped = field.reshape(VARS, N_GX, CX, N_GY, CY, CZ).transpose(1, 3, 0, 2, 4, 5)
    return shaped.reshape(DEVICES, VARS, CELLS)


def from_blocks(blocks):
    shaped = blocks.reshape(N_GX, N_GY, VARS, CX, CY, CZ).transpose(2, 0, 3, 1, 4, 5)
    return shaped.reshape(VARS, NX, NY, CZ)


def reference(q_now, q_prev, jacobian, flux_split, donor_base, donor_frac, fringe_dest, receptor_cell, fringe_count):
    row_ids = jnp.arange(ROWS, dtype=jnp.int32)
    sender = row_ids // F_DEV
    live = ((row_ids % F_DEV) < fringe_count[sender]).astype(jnp.float32)
    dest = fringe_dest[:, 0]
    base_z = donor_base % (CZ - 1)
    base_y = (donor_base // (CZ - 1)) % (CY - 1)
    base_x = donor_base // ((CZ - 1) * (CY - 1))
    corners = []
    for i in range(2):
        for j in range(2):
            for k in range(2):
                index = ((base_x + i) * CY + base_y + j) * CZ + base_z + k
                weight = (donor_frac[0] if i else 1.0 - donor_frac[0])
                weight = weight * (donor_frac[1] if j else 1.0 - donor_frac[1])
                weight = weight * (donor_frac[2] if k else 1.0 - donor_frac[2])
                corners.append((index.astype(jnp.int32), weight))
    hits = jnp.zeros((DEVICES, CELLS), jnp.float32).at[dest, receptor_cell].add(live)
    hits = hits.reshape(N_GX, N_GY, CX, CY, CZ).transpose(0, 2, 1, 3, 4).reshape(NX, NY, CZ)
    state = q_now
    lagged = q_prev
    for step in range(SUBITERS):
        blocks = to_blocks(lagged)
        values = jnp.zeros((ROWS, VARS), jnp.float32)
        for index, weight in corners:
            values = values + weight[:, None] * blocks[sender, :, index]
        values = values * live[:, None]
        landed = jnp.zeros((DEVICES, VARS, CELLS), jnp.float32).at[dest, :, receptor_cell].add(values)
        target = from_blocks(landed)
        lagged = state
        padded = jnp.pad(state, ((0, 0), (1, 1), (1, 1), (1, 1)))
        flux = residual_padded(padded, flux_split)
        physical = (3.0 * state - 4.0 * q_now + q_prev) / (2.0 * step_phys)
        coupling = penalty * (hits[None] * state - target)
        state = state - step_tau * jacobian[None] * (flux + physical + coupling)
    return state
```

```python
import jax
import jax.numpy as jnp
from jax import lax
from jax.experimental import pallas as pl
from jax.experimental.pallas import tpu as pltpu
from jax.sharding import PartitionSpec as P

MESH = pl.DeviceIdType.MESH
F32 = jnp.float32
BF16 = jnp.bfloat16
V, CX, CY, CZ = 5, 16, 16, 256
ROWS = 1024
NDEV = 128
CAP = 16
GX, GY = 8, 16
VY = V * CY
CHUNK = 256
LIMIT = 48 * 1024 * 1024


def iota(shape, dim):
    return lax.broadcasted_iota(jnp.int32, shape, dim)


def two(a):
    hi = a.astype(BF16)
    return hi, (a - hi.astype(F32)).astype(BF16)


def dot(a, b):
    return lax.dot_general(a, b, (((1,), (0,)), ((), ())), preferred_element_type=F32)


def dot_t(a, b):
    return lax.dot_general(a, b, (((1,), (1,)), ((), ())), preferred_element_type=F32)


def flux_matrix(flux):
    col = iota((1, 256), 1)
    block = (col >= 80).astype(jnp.int32) + (col >= 160).astype(jnp.int32) + (col >= 240).astype(jnp.int32)
    side = (col >= 248).astype(jnp.int32)
    var = jnp.where(block == 3, col - 240 - 8 * side, (col >> 4) - 5 * block)
    yc = jnp.where(block == 3, 17 * side - 1, col & 15)
    y = iota((CY, 256), 0)
    here = (yc == y).astype(F32)
    back = (yc == y - 1).astype(F32)
    fwd = (yc == y + 1).astype(F32)
    mid = (block == 1).astype(F32)
    near = ((block == 1) | (block == 3)).astype(F32)
    w_mid, w_back, w_fwd = here * mid, back * near, fwd * near
    w_left, w_right = here * (block == 0).astype(F32), here * (block == 2).astype(F32)
    mains, ups, downs = [], [], []
    for a in range(V):
        row = {}
        for d in range(3):
            for s in range(2):
                total = jnp.zeros((1, 256), F32)
                for b in range(V):
                    total = jnp.where(var == b, flux[((d * 2 + s) * V + a) * V + b], total)
                row[d, s] = total
        centre = (row[0, 0] - row[0, 1]) + (row[1, 0] - row[1, 1]) + (row[2, 0] - row[2, 1])
        mains.append(
            centre * w_mid - row[1, 0] * w_back + row[1, 1] * w_fwd - row[0, 0] * w_left + row[0, 1] * w_right
        )
        ups.append(row[2, 1] * w_mid)
        downs.append(row[2, 0] * w_mid)
    return jnp.concatenate(mains + ups + downs, axis=0)


def y_faces(planes):
    n = planes[0].shape[0]
    pad = [jnp.zeros((n, 8 - V, CZ), F32)]
    return [jnp.concatenate([p[:, y : y + 1, :] for p in planes] + pad, axis=1) for y in (0, CY - 1)]


def donate(count, flux, q_now, q_prev, base, frac, dest, cell, out, face_x, face_y, km_hi, km_lo, qq):
    planes = [q_now[v] for v in range(V)]
    lo_y, hi_y = y_faces(planes)
    face_y[0] = lo_y
    face_y[1] = hi_y
    for v in range(V):
        face_x[0, v * CY : (v + 1) * CY, :] = q_now[v, 0]
        face_x[1, v * CY : (v + 1) * CY, :] = q_now[v, CX - 1]
    hi, lo = two(flux_matrix(flux))
    km_hi[...] = hi
    km_lo[...] = lo
    for f, ref in enumerate((q_prev, q_now)):
        for v in range(V):
            hi, lo = two(ref[v].reshape(CX * CY, CZ))
            qq[f * V + v, :, 0:CZ] = hi
            qq[f * V + v, :, CZ:] = lo

    live = iota((1, ROWS), 1) < count[0]
    where_to = jnp.where(live, dest[...], NDEV)
    onehot = (iota((NDEV, ROWS), 0) == where_to).astype(F32)
    onehot_b = onehot.astype(BF16)
    before = (iota((CHUNK, CHUNK), 0) < iota((CHUNK, CHUNK), 1)).astype(F32).astype(BF16)
    ones = jnp.ones((CHUNK, CHUNK), BF16)
    carry = jnp.zeros((NDEV, CHUNK), F32)
    slots = []
    for c in range(ROWS // CHUNK):
        part = onehot_b[:, c * CHUNK : (c + 1) * CHUNK]
        rank = dot(part, before) + carry
        carry = carry + dot(part, ones)
        slots.append(jnp.sum(rank * onehot[:, c * CHUNK : (c + 1) * CHUNK], axis=0, keepdims=True))

    packed = jnp.zeros((22 * CAP, NDEV), F32)
    for c in range(ROWS // CHUNK):
        span = slice(c * CHUNK, (c + 1) * CHUNK)
        low = base[:, span]
        base_x = low // ((CZ - 1) * (CY - 1))
        rest = low - base_x * ((CZ - 1) * (CY - 1))
        base_y = rest // (CZ - 1)
        base_z = rest - base_y * (CZ - 1)
        fx, fy, fz = frac[0:1, span], frac[1:2, span], frac[2:3, span]

        def hat(n, low, f, rest):
            at = iota((n, CHUNK), 0)
            return jnp.where(at == low, rest, jnp.where(at == low + 1, f, jnp.zeros_like(f)))

        z_hi, z_lo = two(hat(CZ, base_z, fz, 1.0 - fz))
        w_x, w_y = hat(CX, base_x, fx, 1.0 - fx), hat(CY, base_y, fy, 1.0 - fy)
        w_xy = jnp.concatenate([w_x[x : x + 1] * w_y for x in range(CX)], axis=0)
        values = []
        for f in range(2):
            left = qq[f * V : (f + 1) * V].reshape(V * CX * CY, 2 * CZ)
            along = dot(left, jnp.concatenate([z_hi, z_hi], axis=0)) + dot(left[:, 0:CZ], z_lo)
            for v in range(V):
                values.append(jnp.sum(along[v * 256 : (v + 1) * 256] * w_xy, axis=0, keepdims=True))
        cells = cell[:, span]
        rows_hi, rows_lo = [], []
        at_slot = (iota((CAP, CHUNK), 0).astype(F32) == slots[c]).astype(F32)
        for value in values:
            hi = value.astype(BF16).astype(F32)
            rows_hi.append((at_slot * hi).astype(BF16))
            rows_lo.append((at_slot * (value - hi)).astype(BF16))
        xy = ((cells >> 8) + 1).astype(F32)
        z = (cells & 255).astype(F32)
        left = jnp.concatenate(
            rows_hi + [(at_slot * xy).astype(BF16), (at_slot * z).astype(BF16)] + rows_lo, axis=0
        )
        packed = packed + dot_t(left, onehot_b[:, span])
    half = 2 * V * CAP
    full = jnp.concatenate(
        [packed[:half] + packed[half + 2 * CAP :], packed[half : half + 2 * CAP], jnp.zeros((4 * CAP, NDEV), F32)], axis=0
    )
    for h in range(2):
        out[:, :, h, :] = full[h * 128 : (h + 1) * 128].T.reshape(GX, GY, 128)


def split_planes(qs_hi, qs_lo, halo_x, halo_y, hs_hi, hs_lo):
    ix, iy = lax.axis_index("gx"), lax.axis_index("gy")
    nx, ny = lax.axis_size("gx"), lax.axis_size("gy")
    for side, plane, there in ((0, 0, ix > 0), (1, CX + 1, ix < nx - 1)):
        keep = jnp.where(there, 1.0, 0.0)
        hi, lo = two(halo_x[side] * keep)
        qs_hi[plane] = hi
        qs_lo[plane] = lo
    keep = [jnp.where(iy > 0, 1.0, 0.0), jnp.where(iy < ny - 1, 1.0, 0.0)]
    hi, lo = two(jnp.concatenate([halo_y[side] * keep[side] for side in range(2)], axis=1))
    hs_hi[...] = hi
    hs_lo[...] = lo


def flux_of(x, km_hi, km_lo, qs_hi, qs_lo, hs_hi, hs_lo):
    right_hi = jnp.concatenate([qs_hi[x], qs_hi[x + 1], qs_hi[x + 2], hs_hi[x]], axis=0)
    right_lo = jnp.concatenate([qs_lo[x], qs_lo[x + 1], qs_lo[x + 2], hs_lo[x]], axis=0)
    total = dot(km_hi[...], right_hi) + dot(km_lo[...], right_hi) + dot(km_hi[...], right_lo)
    z = iota((VY, CZ), 1)
    fwd = jnp.where(z == CZ - 1, 0.0, pltpu.roll(total[VY : 2 * VY], CZ - 1, 1))
    back = jnp.where(z == 0, 0.0, pltpu.roll(total[2 * VY :], 1, 1))
    return total[:VY] + fwd - back


def first(got, q_now, q_prev, jac, halo_x, halo_y, km_hi, km_lo, state, later, face_x, face_y,
          qs_hi, qs_lo, hs_hi, hs_lo, parts, places, at_z):
    for x in range(CX):
        for v in range(V):
            hi, lo = two(q_now[v, x])
            qs_hi[x + 1, v * CY : (v + 1) * CY, :] = hi
            qs_lo[x + 1, v * CY : (v + 1) * CY, :] = lo
    split_planes(qs_hi, qs_lo, halo_x, halo_y, hs_hi, hs_lo)

    halves = [got[:, :, h, :].reshape(NDEV, 128) for h in range(2)]
    turned = jnp.concatenate([h.T for h in halves], axis=0)
    for s in range(CAP):
        lanes = slice(s * NDEV, (s + 1) * NDEV)
        for g in range(2):
            for v in range(V):
                row = turned[(g * V + v) * CAP + s :][:1]
                hi, lo = two(jnp.broadcast_to(row, (CY, NDEV)))
                parts[g * 11 + v, :, lanes] = hi
                parts[g * 11 + V + v, :, lanes] = lo
        parts[10, :, lanes] = jnp.ones((CY, NDEV), BF16)
        places[:, lanes] = jnp.broadcast_to(turned[10 * CAP + s :][:1], (CY, NDEV))
        column = halves[1][:, 3 * CAP + s : 3 * CAP + s + 1]
        at_z[lanes, :] = (iota((NDEV, CZ), 1).astype(F32) == column).astype(F32).astype(BF16)

    def plane(x, carry):
        mark = (iota((CY, 1), 0) + (x * CY + 1)).astype(F32)
        here = (places[...] == mark).astype(F32).astype(BF16)
        left = jnp.concatenate([parts[i] * here for i in range(21)], axis=0)
        landed = dot(left, at_z[...])
        flux = flux_of(x, km_hi, km_lo, qs_hi, qs_lo, hs_hi, hs_lo)
        scale = 0.2 * jac[x]
        hits = landed[10 * CY : 11 * CY]
        fresh = []
        for v in range(V):
            rows = slice(v * CY, (v + 1) * CY)
            q, qp = q_now[v, x], q_prev[v, x]
            g1 = landed[v * CY : (v + 1) * CY] + landed[(V + v) * CY : (V + v + 1) * CY]
            g2 = landed[(11 + v) * CY : (12 + v) * CY] + landed[(16 + v) * CY : (17 + v) * CY]
            w = q - scale * (flux[rows] + (qp - q) + 2.0 * (hits * q - g1))
            state[x, rows, :] = w
            later[x, rows, :] = w - scale * ((3.0 * w - 4.0 * q + qp) + 2.0 * (hits * w - g2))
            fresh.append(w[None])
        lo_y, hi_y = y_faces(fresh)
        face_y[0, x] = lo_y[0]
        face_y[1, x] = hi_y[0]
        return carry

    lax.fori_loop(0, CX, plane, 0)
    face_x[0] = state[0]
    face_x[1] = state[CX - 1]


def second(state, later, jac, halo_x, halo_y, km_hi, km_lo, out, qs_hi, qs_lo, hs_hi, hs_lo):
    for x in range(CX):
        hi, lo = two(state[x])
        qs_hi[x + 1] = hi
        qs_lo[x + 1] = lo
    split_planes(qs_hi, qs_lo, halo_x, halo_y, hs_hi, hs_lo)

    def plane(x, carry):
        flux = flux_of(x, km_hi, km_lo, qs_hi, qs_lo, hs_hi, hs_lo)
        scale = 0.2 * jac[x]
        for v in range(V):
            rows = slice(v * CY, (v + 1) * CY)
            out[v, x] = later[x, rows, :] - scale * flux[rows]
        return carry

    lax.fori_loop(0, CX, plane, 0)


def face_copies(ix, iy, face_x, face_y, halo_x, halo_y, send, recv):
    copies = []
    for side in range(2):
        step = 2 * side - 1
        peer_x = lax.rem(ix + step + GX, GX)
        peer_y = lax.rem(iy + step + GY, GY)
        copies.append(
            pltpu.make_async_remote_copy(
                face_x.at[side], halo_x.at[1 - side], send.at[side], recv.at[side],
                device_id=(peer_x, iy), device_id_type=MESH,
            )
        )
        copies.append(
            pltpu.make_async_remote_copy(
                face_y.at[side], halo_y.at[1 - side], send.at[2 + side], recv.at[2 + side],
                device_id=(ix, peer_y), device_id_type=MESH,
            )
        )
    return copies


def exchange(sent, face_x, face_y, got, halo_x, halo_y, mid, send, recv, send_a, recv_a, send_b, recv_b):
    ix, iy = lax.axis_index("gx"), lax.axis_index("gy")
    peers = [(lax.rem(ix + k, GX), iy) for k in range(1, GX)] + [(ix, lax.rem(iy + k, GY)) for k in range(1, GY)]
    barrier = pltpu.get_barrier_semaphore()
    for peer in peers:
        pl.semaphore_signal(barrier, inc=1, device_id=peer, device_id_type=MESH)
    pl.semaphore_wait(barrier, len(peers))
    along = []
    for k in range(1, GX):
        to = lax.rem(ix + k, GX)
        copy = pltpu.make_async_remote_copy(
            sent.at[to], mid.at[ix], send_a.at[k - 1], recv_a.at[k - 1], device_id=(to, iy), device_id_type=MESH
        )
        copy.start()
        along.append(copy)
    faces = face_copies(ix, iy, face_x, face_y, halo_x, halo_y, send, recv)
    for copy in faces:
        copy.start()
    mid[ix] = sent[ix]
    for copy in along:
        copy.wait_recv()
    across = []
    for k in range(1, GY):
        to = lax.rem(iy + k, GY)
        copy = pltpu.make_async_remote_copy(
            mid.at[:, to], got.at[iy], send_b.at[k - 1], recv_b.at[k - 1], device_id=(ix, to), device_id_type=MESH
        )
        copy.start()
        across.append(copy)
    got[iy] = mid[:, iy]
    for copy in along:
        copy.wait_send()
    for copy in faces + across:
        copy.wait()


def neighbours(face_x, face_y, halo_x, halo_y, send, recv):
    ix, iy = lax.axis_index("gx"), lax.axis_index("gy")
    barrier = pltpu.get_barrier_semaphore()
    for step in (-1, 1):
        for peer in ((lax.rem(ix + step + GX, GX), iy), (ix, lax.rem(iy + step + GY, GY))):
            pl.semaphore_signal(barrier, inc=1, device_id=peer, device_id_type=MESH)
    pl.semaphore_wait(barrier, 4)
    faces = face_copies(ix, iy, face_x, face_y, halo_x, halo_y, send, recv)
    for copy in faces:
        copy.start()
    for copy in faces:
        copy.wait()


VM = pl.BlockSpec(memory_space=pltpu.VMEM)
SM = pl.BlockSpec(memory_space=pltpu.SMEM)
FACES = [jax.ShapeDtypeStruct((2, VY, CZ), F32), jax.ShapeDtypeStruct((2, CX, 8, CZ), F32)]
MATRIX = [jax.ShapeDtypeStruct((3 * VY, 256), BF16)] * 2
PLANES = [pltpu.VMEM((CX + 2, VY, CZ), BF16)] * 2 + [pltpu.VMEM((CX, 16, CZ), BF16)] * 2


def call_donate(count, flux, q_now, q_prev, base, frac, dest, cell):
    return pl.pallas_call(
        donate,
        out_shape=[jax.ShapeDtypeStruct((GX, GY, 2, 128), F32)] + FACES + MATRIX,
        in_specs=[SM, SM] + [VM] * 6,
        out_specs=[VM] * 5,
        scratch_shapes=[pltpu.VMEM((2 * V, CX * CY, 2 * CZ), BF16)],
        compiler_params=pltpu.CompilerParams(vmem_limit_bytes=LIMIT),
        name="donate",
    )(count, flux, q_now, q_prev, base, frac, dest, cell)


def call_exchange(sent, face_x, face_y):
    return pl.pallas_call(
        exchange,
        out_shape=[jax.ShapeDtypeStruct((GY, GX, 2, 128), F32)] + FACES,
        in_specs=[VM] * 3,
        out_specs=[VM] * 3,
        scratch_shapes=[pltpu.VMEM((GX, GY, 2, 128), F32)]
        + [pltpu.SemaphoreType.DMA((4,))] * 2
        + [pltpu.SemaphoreType.DMA((GX - 1,))] * 2
        + [pltpu.SemaphoreType.DMA((GY - 1,))] * 2,
        compiler_params=pltpu.CompilerParams(vmem_limit_bytes=LIMIT, collective_id=0, has_side_effects=True),
        name="exchange",
    )(sent, face_x, face_y)


def call_first(got, q_now, q_prev, jac, halo_x, halo_y, km_hi, km_lo):
    return pl.pallas_call(
        first,
        out_shape=[jax.ShapeDtypeStruct((CX, VY, CZ), F32)] * 2 + FACES,
        in_specs=[VM] * 8,
        out_specs=[VM] * 4,
        scratch_shapes=PLANES
        + [
            pltpu.VMEM((21, CY, NDEV * CAP), BF16),
            pltpu.VMEM((CY, NDEV * CAP), F32),
            pltpu.VMEM((NDEV * CAP, CZ), BF16),
        ],
        compiler_params=pltpu.CompilerParams(vmem_limit_bytes=LIMIT),
        name="first",
    )(got, q_now, q_prev, jac, halo_x, halo_y, km_hi, km_lo)


def call_neighbours(face_x, face_y):
    return pl.pallas_call(
        neighbours,
        out_shape=FACES,
        in_specs=[VM] * 2,
        out_specs=[VM] * 2,
        scratch_shapes=[pltpu.SemaphoreType.DMA((4,))] * 2,
        compiler_params=pltpu.CompilerParams(vmem_limit_bytes=LIMIT, collective_id=1, has_side_effects=True),
        name="neighbours",
    )(face_x, face_y)


def call_second(state, later, jac, halo_x, halo_y, km_hi, km_lo):
    return pl.pallas_call(
        second,
        out_shape=jax.ShapeDtypeStruct((V, CX, CY, CZ), F32),
        in_specs=[VM] * 7,
        out_specs=VM,
        scratch_shapes=PLANES,
        compiler_params=pltpu.CompilerParams(vmem_limit_bytes=LIMIT),
        name="second",
    )(state, later, jac, halo_x, halo_y, km_hi, km_lo)


def body(q_now, q_prev, jacobian, flux_split, donor_base, donor_frac, fringe_dest, receptor_cell, fringe_count):
    sent, face_x, face_y, km_hi, km_lo = call_donate(
        fringe_count, flux_split.reshape(-1), q_now, q_prev, donor_base.reshape(1, ROWS), donor_frac,
        fringe_dest.reshape(1, ROWS), receptor_cell.reshape(1, ROWS),
    )
    got, halo_x, halo_y = call_exchange(sent, face_x, face_y)
    state, later, face_x, face_y = call_first(got, q_now, q_prev, jacobian, halo_x, halo_y, km_hi, km_lo)
    halo_x, halo_y = call_neighbours(face_x, face_y)
    return call_second(state, later, jacobian, halo_x, halo_y, km_hi, km_lo)


def solution(mesh):
    return jax.shard_map(
        body,
        mesh=mesh,
        in_specs=(
            P(None, "gx", "gy", None),
            P(None, "gx", "gy", None),
            P("gx", "gy", None),
            P(),
            P(("gx", "gy")),
            P(None, ("gx", "gy")),
            P(("gx", "gy"), None),
            P(("gx", "gy")),
            P(("gx", "gy")),
        ),
        out_specs=P(None, "gx", "gy", None),
        check_vma=False,
    )
```

```python
import jax
import jax.numpy as jnp
from jax import lax
from jax.experimental import pallas as pl
from jax.experimental.pallas import tpu as pltpu
from jax.sharding import PartitionSpec as P

MESH = pl.DeviceIdType.MESH
F32 = jnp.float32
BF16 = jnp.bfloat16
V, CX, CY, CZ = 5, 16, 16, 256
ROWS = 1024
NDEV = 128
CAP = 16
GX, GY = 8, 16
VY = V * CY
CHUNK = 256
GROUP = 4
LIMIT = 48 * 1024 * 1024


def iota(shape, dim):
    return lax.broadcasted_iota(jnp.int32, shape, dim)


def two(a):
    hi = a.astype(BF16)
    return hi, (a - hi.astype(F32)).astype(BF16)


def dot(a, b):
    return lax.dot_general(a, b, (((1,), (0,)), ((), ())), preferred_element_type=F32)


def dot_t(a, b):
    return lax.dot_general(a, b, (((1,), (1,)), ((), ())), preferred_element_type=F32)


def flux_matrix(flux):
    col = iota((1, 256), 1)
    block = (col >= 80).astype(jnp.int32) + (col >= 160).astype(jnp.int32) + (col >= 240).astype(jnp.int32)
    side = (col >= 248).astype(jnp.int32)
    var = jnp.where(block == 3, col - 240 - 8 * side, (col >> 4) - 5 * block)
    yc = jnp.where(block == 3, 17 * side - 1, col & 15)
    y = iota((CY, 256), 0)
    here = (yc == y).astype(F32)
    back = (yc == y - 1).astype(F32)
    fwd = (yc == y + 1).astype(F32)
    mid = (block == 1).astype(F32)
    near = ((block == 1) | (block == 3)).astype(F32)
    w_mid, w_back, w_fwd = here * mid, back * near, fwd * near
    w_left, w_right = here * (block == 0).astype(F32), here * (block == 2).astype(F32)
    mains, ups, downs = [], [], []
    for a in range(V):
        row = {}
        for d in range(3):
            for s in range(2):
                total = jnp.zeros((1, 256), F32)
                for b in range(V):
                    total = jnp.where(var == b, flux[d, a, s : s + 1, b : b + 1], total)
                row[d, s] = total
        centre = (row[0, 0] - row[0, 1]) + (row[1, 0] - row[1, 1]) + (row[2, 0] - row[2, 1])
        mains.append(
            centre * w_mid - row[1, 0] * w_back + row[1, 1] * w_fwd - row[0, 0] * w_left + row[0, 1] * w_right
        )
        ups.append(row[2, 1] * w_mid)
        downs.append(row[2, 0] * w_mid)
    return jnp.concatenate(mains + ups + downs, axis=0)


def y_faces(planes):
    pad = [jnp.zeros((8 - V, CZ), F32)]
    return [jnp.concatenate([p[y : y + 1, :] for p in planes] + pad, axis=0) for y in (0, CY - 1)]


def beyond(halo_x, halo_y):
    ix, iy = lax.axis_index("gx"), lax.axis_index("gy")
    nx, ny = lax.axis_size("gx"), lax.axis_size("gy")
    keep_x = [jnp.where(ix > 0, 1.0, 0.0), jnp.where(ix < nx - 1, 1.0, 0.0)]
    keep_y = [jnp.where(iy > 0, 1.0, 0.0), jnp.where(iy < ny - 1, 1.0, 0.0)]
    ends = [two(halo_x[side] * keep_x[side]) for side in range(2)]
    rows = [
        two(jnp.concatenate([halo_y[side, x] * keep_y[side] for side in range(2)], axis=0)) for x in range(CX)
    ]
    return ends, rows


def flux_of(x, km_hi, km_lo, hi, lo, ends, rows):
    def tile(ref, part):
        left = ends[0][part] if x == 0 else ref[x - 1]
        right = ends[1][part] if x == CX - 1 else ref[x + 1]
        return jnp.concatenate([left, ref[x], right, rows[x][part]], axis=0)

    top, low = tile(hi, 0), tile(lo, 1)
    total = dot(km_hi[...], top) + dot(km_lo[...], top) + dot(km_hi[...], low)
    z = iota((VY, CZ), 1)
    fwd = jnp.where(z == CZ - 1, 0.0, pltpu.roll(total[VY : 2 * VY], CZ - 1, 1))
    back = jnp.where(z == 0, 0.0, pltpu.roll(total[2 * VY :], 1, 1))
    return total[:VY] + fwd - back


def face_copies(ix, iy, face_x, face_y, halo_x, halo_y, send, recv):
    copies = []
    for side in range(2):
        step = 2 * side - 1
        peer_x = lax.rem(ix + step + GX, GX)
        peer_y = lax.rem(iy + step + GY, GY)
        copies.append(
            pltpu.make_async_remote_copy(
                face_x.at[side], halo_x.at[1 - side], send.at[side], recv.at[side],
                device_id=(peer_x, iy), device_id_type=MESH,
            )
        )
        copies.append(
            pltpu.make_async_remote_copy(
                face_y.at[side], halo_y.at[1 - side], send.at[2 + side], recv.at[2 + side],
                device_id=(ix, peer_y), device_id_type=MESH,
            )
        )
    return copies


def ranks(onehot, onehot_b):
    before = (iota((CHUNK, CHUNK), 0) < iota((CHUNK, CHUNK), 1)).astype(F32).astype(BF16)
    ones = jnp.ones((CHUNK, CHUNK), BF16)
    carry = jnp.zeros((NDEV, CHUNK), F32)
    slots = []
    for c in range(ROWS // CHUNK):
        part = onehot_b[:, c * CHUNK : (c + 1) * CHUNK]
        rank = dot(part, before) + carry
        carry = carry + dot(part, ones)
        slots.append(jnp.sum(rank * onehot[:, c * CHUNK : (c + 1) * CHUNK], axis=0, keepdims=True))
    return slots


def hat(n, low, f):
    at = iota((n, CHUNK), 0)
    return jnp.where(at == low, 1.0 - f, jnp.where(at == low + 1, f, jnp.zeros_like(f)))


def pack(base, frac, cell, slots, onehot_b, fields):
    packed = jnp.zeros((22 * CAP, NDEV), F32)
    for c in range(ROWS // CHUNK):
        span = slice(c * CHUNK, (c + 1) * CHUNK)
        low = base[:, span]
        base_x = low // ((CZ - 1) * (CY - 1))
        rest = low - base_x * ((CZ - 1) * (CY - 1))
        base_y = rest // (CZ - 1)
        base_z = rest - base_y * (CZ - 1)
        fx, fy, fz = frac[0:1, span], frac[1:2, span], frac[2:3, span]
        z_hi, z_lo = two(hat(CZ, base_z, fz))
        w_x, w_y = hat(CX, base_x, fx), hat(CY, base_y, fy)
        w_xy = [w_x[x : x + 1] * w_y for x in range(CX)]
        right = jnp.concatenate([z_hi, z_hi, z_lo], axis=0)
        values = []
        for hi, lo in fields:
            top, rem = hi[...].reshape(CX * VY, CZ), lo[...].reshape(CX * VY, CZ)
            along = dot(jnp.concatenate([top, rem, top], axis=1), right)
            for v in range(V):
                total = jnp.zeros((CY, CHUNK), F32)
                for x in range(CX):
                    at = x * VY + v * CY
                    total = total + along[at : at + CY] * w_xy[x]
                values.append(jnp.sum(total, axis=0, keepdims=True))
        cells = cell[:, span]
        rows_hi, rows_lo = [], []
        at_slot = (iota((CAP, CHUNK), 0).astype(F32) == slots[c]).astype(F32)
        for value in values:
            hi = value.astype(BF16).astype(F32)
            rows_hi.append((at_slot * hi).astype(BF16))
            rows_lo.append((at_slot * (value - hi)).astype(BF16))
        xy = ((cells >> 8) + 1).astype(F32)
        z = (cells & 255).astype(F32)
        left = jnp.concatenate(
            rows_hi + [(at_slot * xy).astype(BF16), (at_slot * z).astype(BF16)] + rows_lo, axis=0
        )
        packed = packed + dot_t(left, onehot_b[:, span])
    half = 2 * V * CAP
    return jnp.concatenate(
        [packed[:half] + packed[half + 2 * CAP :], packed[half : half + 2 * CAP], jnp.zeros((4 * CAP, NDEV), F32)], axis=0
    )


def launch(count, flux_h, now_h, prev_h, jac_h, base_h, frac_h, dest_h, cell_h, got, start, km_hi, km_lo,
           flux, q_now, q_prev, jac, base, frac, dest, cell, now_hi, now_lo, prev_hi, prev_lo, sent, mid,
           face_x, face_y, halo_x, halo_y, load, send, recv, send_a, recv_a, send_b, recv_b):
    loads = [
        pltpu.make_async_copy(a, b, load.at[i])
        for i, (a, b) in enumerate(
            [(dest_h, dest), (flux_h, flux), (base_h, base), (frac_h, frac), (cell_h, cell),
             (prev_h, q_prev), (now_h, q_now), (jac_h, jac)]
        )
    ]
    for copy in loads:
        copy.start()
    ix, iy = lax.axis_index("gx"), lax.axis_index("gy")
    peers = [(lax.rem(ix + k, GX), iy) for k in range(1, GX)] + [(ix, lax.rem(iy + k, GY)) for k in range(1, GY)]
    barrier = pltpu.get_barrier_semaphore()
    for peer in peers:
        pl.semaphore_signal(barrier, inc=1, device_id=peer, device_id_type=MESH)

    loads[0].wait()
    live = iota((1, ROWS), 1) < count[0]
    where_to = jnp.where(live, dest[...], NDEV)
    onehot = (iota((NDEV, ROWS), 0) == where_to).astype(F32)
    onehot_b = onehot.astype(BF16)
    slots = ranks(onehot, onehot_b)
    for copy in loads[1:]:
        copy.wait()
    for x in range(CX):
        for v in range(V):
            for ref, top, low in ((q_prev, prev_hi, prev_lo), (q_now, now_hi, now_lo)):
                hi, lo = two(ref[v, x])
                top[x, v * CY : (v + 1) * CY, :] = hi
                low[x, v * CY : (v + 1) * CY, :] = lo
        lo_y, hi_y = y_faces([q_now[v, x] for v in range(V)])
        face_y[0, x] = lo_y
        face_y[1, x] = hi_y
    for v in range(V):
        face_x[0, v * CY : (v + 1) * CY, :] = q_now[v, 0]
        face_x[1, v * CY : (v + 1) * CY, :] = q_now[v, CX - 1]
    full = pack(base, frac, cell, slots, onehot_b, ((prev_hi, prev_lo), (now_hi, now_lo)))
    for h in range(2):
        sent[:, :, h, :] = full[h * 128 : (h + 1) * 128].T.reshape(GX, GY, 128)

    pl.semaphore_wait(barrier, len(peers))
    along = []
    for k in range(1, GX):
        to = lax.rem(ix + k, GX)
        copy = pltpu.make_async_remote_copy(
            sent.at[to], mid.at[ix], send_a.at[k - 1], recv_a.at[k - 1], device_id=(to, iy), device_id_type=MESH
        )
        copy.start()
        along.append(copy)
    faces = face_copies(ix, iy, face_x, face_y, halo_x, halo_y, send, recv)
    for copy in faces:
        copy.start()
    mid[ix] = sent[ix]
    hi, lo = two(flux_matrix(flux))
    km_hi[...] = hi
    km_lo[...] = lo
    for copy in along:
        copy.wait_recv()
    across = []
    for k in range(1, GY):
        to = lax.rem(iy + k, GY)
        copy = pltpu.make_async_remote_copy(
            mid.at[:, to], got.at[iy], send_b.at[k - 1], recv_b.at[k - 1], device_id=(ix, to), device_id_type=MESH
        )
        copy.start()
        across.append(copy)
    got[iy] = mid[:, iy]
    for copy in along:
        copy.wait_send()
    for copy in faces:
        copy.wait()
    ends, rows = beyond(halo_x, halo_y)
    for x in range(CX):
        flux_x = flux_of(x, km_hi, km_lo, now_hi, now_lo, ends, rows)
        scale = 0.2 * jac[x]
        for v in range(V):
            part = slice(v * CY, (v + 1) * CY)
            start[x, part, :] = q_now[v, x] - scale * (flux_x[part] + (q_prev[v, x] - q_now[v, x]))
    for copy in across:
        copy.wait()


def settle(got, start, q_now, q_prev, jac, later, hi_out, lo_out, halo_x, halo_y,
           face_x, face_y, parts, places, at_z, send, recv):
    ix, iy = lax.axis_index("gx"), lax.axis_index("gy")
    barrier = pltpu.get_barrier_semaphore()
    for step in (-1, 1):
        for peer in ((lax.rem(ix + step + GX, GX), iy), (ix, lax.rem(iy + step + GY, GY))):
            pl.semaphore_signal(barrier, inc=1, device_id=peer, device_id_type=MESH)

    halves = [got[:, :, h, :].reshape(NDEV, 128) for h in range(2)]
    turned = jnp.concatenate([h.T for h in halves], axis=0)
    for s in range(CAP):
        lanes = slice(s * NDEV, (s + 1) * NDEV)
        for g in range(2):
            for v in range(V):
                row = turned[(g * V + v) * CAP + s :][:1]
                hi, lo = two(jnp.broadcast_to(row, (CY, NDEV)))
                parts[g * 11 + v, :, lanes] = hi
                parts[g * 11 + V + v, :, lanes] = lo
        parts[10, :, lanes] = jnp.ones((CY, NDEV), BF16)
        places[:, lanes] = jnp.broadcast_to(turned[10 * CAP + s :][:1], (CY, NDEV))
        column = halves[1][:, 3 * CAP + s : 3 * CAP + s + 1]
        at_z[lanes, :] = (iota((NDEV, CZ), 1).astype(F32) == column).astype(F32).astype(BF16)

    def landing(group, first, last):
        left = []
        for j in range(GROUP):
            mark = (iota((CY, 1), 0) + ((group * GROUP + j) * CY + 1)).astype(F32)
            here = (places[...] == mark).astype(F32).astype(BF16)
            left += [parts[i] * here for i in range(first, last)]
        return dot(jnp.concatenate(left, axis=0), at_z[...])

    def rows_of(landed, j, n, i):
        return landed[(j * n + i) * CY : (j * n + i + 1) * CY]

    for group in range(CX // GROUP):
        landed = landing(group, 0, 11)
        for j in range(GROUP):
            x = group * GROUP + j
            scale = 0.2 * jac[x]
            hits = rows_of(landed, j, 11, 10)
            fresh = []
            for v in range(V):
                part = slice(v * CY, (v + 1) * CY)
                q, qp = q_now[v, x], q_prev[v, x]
                target = rows_of(landed, j, 11, v) + rows_of(landed, j, 11, V + v)
                w = start[x, part, :] - scale * (2.0 * (hits * q - target))
                hi, lo = two(w)
                hi_out[x, part, :] = hi
                lo_out[x, part, :] = lo
                later[x, part, :] = w - scale * ((3.0 * w - 4.0 * q + qp) + 2.0 * (hits * w))
                fresh.append(w)
                if x in (0, CX - 1):
                    face_x[0 if x == 0 else 1, part, :] = w
            lo_y, hi_y = y_faces(fresh)
            face_y[0, x] = lo_y
            face_y[1, x] = hi_y
    pl.semaphore_wait(barrier, 4)
    faces = face_copies(ix, iy, face_x, face_y, halo_x, halo_y, send, recv)
    for copy in faces:
        copy.start()
    for group in range(CX // GROUP):
        landed = landing(group, 11, 21)
        for j in range(GROUP):
            x = group * GROUP + j
            scale = 0.4 * jac[x]
            for v in range(V):
                part = slice(v * CY, (v + 1) * CY)
                target = rows_of(landed, j, 10, v) + rows_of(landed, j, 10, V + v)
                later[x, part, :] = later[x, part, :] + scale * target
    for copy in faces:
        copy.wait()


def second(hi, lo, later, jac, halo_x, halo_y, km_hi, km_lo, out):
    ends, rows = beyond(halo_x, halo_y)
    for x in range(CX):
        flux = flux_of(x, km_hi, km_lo, hi, lo, ends, rows)
        scale = 0.2 * jac[x]
        for v in range(V):
            part = slice(v * CY, (v + 1) * CY)
            out[v, x] = later[x, part, :] - scale * flux[part]


VM = pl.BlockSpec(memory_space=pltpu.VMEM)
SM = pl.BlockSpec(memory_space=pltpu.SMEM)
HB = pl.BlockSpec(memory_space=pltpu.HBM)
FACES = [((2, VY, CZ), F32), ((2, CX, 8, CZ), F32)]
PLANES = ((CX, VY, CZ), F32)
PARTS = [((CX, VY, CZ), BF16)] * 2
MATRIX = [((3 * VY, 256), BF16)] * 2


def shapes(entries):
    return [jax.ShapeDtypeStruct(*e) for e in entries]


def vmem(entries):
    return [pltpu.VMEM(*e) for e in entries]


def call_launch(count, flux, q_now, q_prev, jac, base, frac, dest, cell):
    ins = [flux, q_now, q_prev, jac, base, frac, dest, cell]
    return pl.pallas_call(
        launch,
        out_shape=shapes([((GY, GX, 2, 128), F32), PLANES] + MATRIX),
        in_specs=[SM] + [HB] * 8,
        out_specs=[VM] * 4,
        scratch_shapes=vmem([(a.shape, a.dtype) for a in ins])
        + vmem(PARTS * 2 + [((GX, GY, 2, 128), F32)] * 2 + FACES * 2)
        + [pltpu.SemaphoreType.DMA((8,))]
        + [pltpu.SemaphoreType.DMA((4,))] * 2
        + [pltpu.SemaphoreType.DMA((GX - 1,))] * 2
        + [pltpu.SemaphoreType.DMA((GY - 1,))] * 2,
        compiler_params=pltpu.CompilerParams(vmem_limit_bytes=LIMIT, collective_id=0, has_side_effects=True),
        name="launch",
    )(count, *ins)


def call_settle(got, start, q_now, q_prev, jac):
    return pl.pallas_call(
        settle,
        out_shape=shapes([PLANES] + PARTS + FACES),
        in_specs=[VM] * 5,
        out_specs=[VM] * 5,
        scratch_shapes=vmem(
            FACES + [((21, CY, NDEV * CAP), BF16), ((CY, NDEV * CAP), F32), ((NDEV * CAP, CZ), BF16)]
        )
        + [pltpu.SemaphoreType.DMA((4,))] * 2,
        compiler_params=pltpu.CompilerParams(vmem_limit_bytes=LIMIT, collective_id=1, has_side_effects=True),
        name="settle",
    )(got, start, q_now, q_prev, jac)


def call_second(hi, lo, later, jac, halo_x, halo_y, km_hi, km_lo):
    return pl.pallas_call(
        second,
        out_shape=jax.ShapeDtypeStruct((V, CX, CY, CZ), F32),
        in_specs=[VM] * 8,
        out_specs=VM,
        compiler_params=pltpu.CompilerParams(vmem_limit_bytes=LIMIT),
        name="second",
    )(hi, lo, later, jac, halo_x, halo_y, km_hi, km_lo)


def body(q_now, q_prev, jacobian, flux_split, donor_base, donor_frac, fringe_dest, receptor_cell, fringe_count):
    got, start, km_hi, km_lo = call_launch(
        fringe_count, flux_split.transpose(0, 2, 1, 3), q_now, q_prev, jacobian, donor_base.reshape(1, ROWS),
        donor_frac, fringe_dest.reshape(1, ROWS), receptor_cell.reshape(1, ROWS),
    )
    later, hi, lo, halo_x, halo_y = call_settle(got, start, q_now, q_prev, jacobian)
    return call_second(hi, lo, later, jacobian, halo_x, halo_y, km_hi, km_lo)


def solution(mesh):
    return jax.shard_map(
        body,
        mesh=mesh,
        in_specs=(
            P(None, "gx", "gy", None),
            P(None, "gx", "gy", None),
            P("gx", "gy", None),
            P(),
            P(("gx", "gy")),
            P(None, ("gx", "gy")),
            P(("gx", "gy"), None),
            P(("gx", "gy")),
            P(("gx", "gy")),
        ),
        out_specs=P(None, "gx", "gy", None),
        check_vma=False,
    )
```

```python
import jax
import jax.numpy as jnp
from jax import lax
from jax.experimental import pallas as pl
from jax.experimental.pallas import tpu as pltpu
from jax.sharding import PartitionSpec as P

MESH = pl.DeviceIdType.MESH
F32 = jnp.float32
BF16 = jnp.bfloat16
V, CX, CY, CZ = 5, 16, 16, 256
ROWS = 1024
NDEV = 128
CAP = 16
GX, GY = 8, 16
VY = V * CY
CHUNK = 256
GROUP = 4
LIMIT = 48 * 1024 * 1024


def iota(shape, dim):
    return lax.broadcasted_iota(jnp.int32, shape, dim)


def two(a):
    hi = a.astype(BF16)
    return hi, (a - hi.astype(F32)).astype(BF16)


def dot(a, b):
    return lax.dot_general(a, b, (((1,), (0,)), ((), ())), preferred_element_type=F32)


def dot_t(a, b):
    return lax.dot_general(a, b, (((1,), (1,)), ((), ())), preferred_element_type=F32)


def flux_matrix(flux):
    col = iota((1, 256), 1)
    block = (col >= 80).astype(jnp.int32) + (col >= 160).astype(jnp.int32) + (col >= 240).astype(jnp.int32)
    side = (col >= 248).astype(jnp.int32)
    var = jnp.where(block == 3, col - 240 - 8 * side, (col >> 4) - 5 * block)
    yc = jnp.where(block == 3, 17 * side - 1, col & 15)
    y = iota((CY, 256), 0)
    here = (yc == y).astype(F32)
    back = (yc == y - 1).astype(F32)
    fwd = (yc == y + 1).astype(F32)
    mid = (block == 1).astype(F32)
    near = ((block == 1) | (block == 3)).astype(F32)
    w_mid, w_back, w_fwd = here * mid, back * near, fwd * near
    w_left, w_right = here * (block == 0).astype(F32), here * (block == 2).astype(F32)
    mains, ups, downs = [], [], []
    for a in range(V):
        row = {}
        for d in range(3):
            for s in range(2):
                total = jnp.zeros((1, 256), F32)
                for b in range(V):
                    total = jnp.where(var == b, flux[d, a, s : s + 1, b : b + 1], total)
                row[d, s] = total
        centre = (row[0, 0] - row[0, 1]) + (row[1, 0] - row[1, 1]) + (row[2, 0] - row[2, 1])
        mains.append(
            centre * w_mid - row[1, 0] * w_back + row[1, 1] * w_fwd - row[0, 0] * w_left + row[0, 1] * w_right
        )
        ups.append(row[2, 1] * w_mid)
        downs.append(row[2, 0] * w_mid)
    return jnp.concatenate(mains + ups + downs, axis=0)


def y_faces(planes):
    pad = [jnp.zeros((8 - V, CZ), F32)]
    return [jnp.concatenate([p[y : y + 1, :] for p in planes] + pad, axis=0) for y in (0, CY - 1)]


def beyond(halo_x, halo_y):
    ix, iy = lax.axis_index("gx"), lax.axis_index("gy")
    nx, ny = lax.axis_size("gx"), lax.axis_size("gy")
    keep_x = [jnp.where(ix > 0, 1.0, 0.0), jnp.where(ix < nx - 1, 1.0, 0.0)]
    keep_y = [jnp.where(iy > 0, 1.0, 0.0), jnp.where(iy < ny - 1, 1.0, 0.0)]
    ends = [two(halo_x[side] * keep_x[side]) for side in range(2)]
    rows = [
        two(jnp.concatenate([halo_y[side, x] * keep_y[side] for side in range(2)], axis=0)) for x in range(CX)
    ]
    return ends, rows


def flux_of(x, km_hi, km_lo, hi, lo, ends, rows):
    def tile(ref, part):
        left = ends[0][part] if x == 0 else ref[x - 1]
        right = ends[1][part] if x == CX - 1 else ref[x + 1]
        return jnp.concatenate([left, ref[x], right, rows[x][part]], axis=0)

    top, low = tile(hi, 0), tile(lo, 1)
    total = dot(km_hi[...], top) + dot(km_lo[...], top) + dot(km_hi[...], low)
    z = iota((VY, CZ), 1)
    fwd = jnp.where(z == CZ - 1, 0.0, pltpu.roll(total[VY : 2 * VY], CZ - 1, 1))
    back = jnp.where(z == 0, 0.0, pltpu.roll(total[2 * VY :], 1, 1))
    return total[:VY] + fwd - back


def face_copies(ix, iy, face_x, face_y, halo_x, halo_y, send, recv):
    copies = []
    for side in range(2):
        step = 2 * side - 1
        peer_x = lax.rem(ix + step + GX, GX)
        peer_y = lax.rem(iy + step + GY, GY)
        copies.append(
            pltpu.make_async_remote_copy(
                face_x.at[side], halo_x.at[1 - side], send.at[side], recv.at[side],
                device_id=(peer_x, iy), device_id_type=MESH,
            )
        )
        copies.append(
            pltpu.make_async_remote_copy(
                face_y.at[side], halo_y.at[1 - side], send.at[2 + side], recv.at[2 + side],
                device_id=(ix, peer_y), device_id_type=MESH,
            )
        )
    return copies


def ranks(onehot, onehot_b):
    before = (iota((CHUNK, CHUNK), 0) < iota((CHUNK, CHUNK), 1)).astype(F32).astype(BF16)
    ones = jnp.ones((CHUNK, CHUNK), BF16)
    carry = jnp.zeros((NDEV, CHUNK), F32)
    slots = []
    for c in range(ROWS // CHUNK):
        part = onehot_b[:, c * CHUNK : (c + 1) * CHUNK]
        rank = dot(part, before) + carry
        carry = carry + dot(part, ones)
        slots.append(jnp.sum(rank * onehot[:, c * CHUNK : (c + 1) * CHUNK], axis=0, keepdims=True))
    return slots


def hat(n, low, f):
    at = iota((n, CHUNK), 0)
    return jnp.where(at == low, 1.0 - f, jnp.where(at == low + 1, f, jnp.zeros_like(f)))


def stencils(base, frac, z_parts, w_xy):
    for c in range(ROWS // CHUNK):
        span = slice(c * CHUNK, (c + 1) * CHUNK)
        low = base[:, span]
        base_x = low // ((CZ - 1) * (CY - 1))
        rest = low - base_x * ((CZ - 1) * (CY - 1))
        base_y = rest // (CZ - 1)
        base_z = rest - base_y * (CZ - 1)
        fx, fy, fz = frac[0:1, span], frac[1:2, span], frac[2:3, span]
        hi, lo = two(hat(CZ, base_z, fz))
        z_parts[c, 0:CZ, :] = hi
        z_parts[c, CZ : 2 * CZ, :] = hi
        z_parts[c, 2 * CZ :, :] = lo
        w_x, w_y = hat(CX, base_x, fx), hat(CY, base_y, fy)
        for x in range(CX):
            w_xy[c, x] = w_x[x : x + 1] * w_y


def donate(c, hi, lo, z_parts, w_xy, slots, onehot_b, extra):
    top, rem = hi[...].reshape(CX * VY, CZ), lo[...].reshape(CX * VY, CZ)
    along = dot(jnp.concatenate([top, rem, top], axis=1), z_parts[c])
    at_slot = (iota((CAP, CHUNK), 0).astype(F32) == slots[c]).astype(F32)
    rows_hi, rows_lo = [], []
    for v in range(V):
        total = jnp.zeros((CY, CHUNK), F32)
        for x in range(CX):
            at = x * VY + v * CY
            total = total + along[at : at + CY] * w_xy[c, x]
        value = jnp.sum(total, axis=0, keepdims=True)
        first = value.astype(BF16).astype(F32)
        rows_hi.append((at_slot * first).astype(BF16))
        rows_lo.append((at_slot * (value - first)).astype(BF16))
    rows_hi += [(at_slot * part.astype(F32)).astype(BF16) for part in extra]
    return dot_t(jnp.concatenate(rows_hi + rows_lo, axis=0), onehot_b[:, c * CHUNK : (c + 1) * CHUNK])


def by_block(packed, extra):
    n, m = V * CAP, (V + extra) * CAP
    rows = [packed[:n] + packed[m:]] + ([packed[n:m]] if extra else []) + [jnp.zeros((128 - m, NDEV), F32)]
    return jnp.concatenate(rows, axis=0).T.reshape(GX, GY, 128)


def advance(count, flux_h, now_h, prev_h, jac_h, base_h, frac_h, dest_h, cell_h,
            later, hi_out, lo_out, halo2_x, halo2_y, km_hi, km_lo,
            flux, q_now, q_prev, jac, base, frac, dest, cell, now_hi, now_lo, prev_hi, prev_lo, start, z_parts, w_xy,
            sent, mid, got, face_x, face_y, halo_x, halo_y, face2_x, face2_y, parts, places, at_z,
            load, send, recv, send2, recv2, send_a, recv_a, send_b, recv_b):
    loads = [
        pltpu.make_async_copy(a, b, load.at[i])
        for i, (a, b) in enumerate(
            [(dest_h, dest), (base_h, base), (frac_h, frac), (prev_h, q_prev), (now_h, q_now), (cell_h, cell),
             (flux_h, flux), (jac_h, jac)]
        )
    ]
    for copy in loads:
        copy.start()
    ix, iy = lax.axis_index("gx"), lax.axis_index("gy")
    peers = [(lax.rem(ix + k, GX), iy) for k in range(1, GX)] + [(ix, lax.rem(iy + k, GY)) for k in range(1, GY)]
    barrier = pltpu.get_barrier_semaphore()
    for peer in peers:
        pl.semaphore_signal(barrier, inc=1, device_id=peer, device_id_type=MESH)

    def along_gx(wave):
        copies = []
        for k in range(1, GX):
            to = lax.rem(ix + k, GX)
            copies.append(
                pltpu.make_async_remote_copy(
                    sent.at[wave, to], mid.at[wave, ix], send_a.at[wave, k - 1], recv_a.at[wave, k - 1],
                    device_id=(to, iy), device_id_type=MESH,
                )
            )
        for copy in copies:
            copy.start()
        mid[wave, ix] = sent[wave, ix]
        return copies

    def along_gy(wave):
        copies = []
        for k in range(1, GY):
            to = lax.rem(iy + k, GY)
            copies.append(
                pltpu.make_async_remote_copy(
                    mid.at[wave, :, to], got.at[wave, iy], send_b.at[wave, k - 1], recv_b.at[wave, k - 1],
                    device_id=(ix, to), device_id_type=MESH,
                )
            )
        for copy in copies:
            copy.start()
        got[wave, iy] = mid[wave, :, iy]
        return copies

    for copy in loads[:3]:
        copy.wait()
    live = iota((1, ROWS), 1) < count[0]
    where_to = jnp.where(live, dest[...], NDEV)
    onehot = (iota((NDEV, ROWS), 0) == where_to).astype(F32)
    onehot_b = onehot.astype(BF16)
    slots = ranks(onehot, onehot_b)
    stencils(base, frac, z_parts, w_xy)
    loads[3].wait()
    loads[5].wait()
    for x in range(CX):
        for v in range(V):
            hi, lo = two(q_prev[v, x])
            prev_hi[x, v * CY : (v + 1) * CY, :] = hi
            prev_lo[x, v * CY : (v + 1) * CY, :] = lo
    packed = jnp.zeros((12 * CAP, NDEV), F32)
    for c in range(ROWS // CHUNK):
        cells = cell[:, c * CHUNK : (c + 1) * CHUNK]
        packed = packed + donate(
            c, prev_hi, prev_lo, z_parts, w_xy, slots, onehot_b, ((cells >> 8) + 1, cells & 255)
        )
    sent[0, :, :, 0, :] = by_block(packed, 2)

    pl.semaphore_wait(barrier, len(peers))
    first_a = along_gx(0)
    for i in (4, 6, 7):
        loads[i].wait()
    for x in range(CX):
        for v in range(V):
            hi, lo = two(q_now[v, x])
            now_hi[x, v * CY : (v + 1) * CY, :] = hi
            now_lo[x, v * CY : (v + 1) * CY, :] = lo
        lo_y, hi_y = y_faces([q_now[v, x] for v in range(V)])
        face_y[0, x] = lo_y
        face_y[1, x] = hi_y
    for v in range(V):
        face_x[0, v * CY : (v + 1) * CY, :] = q_now[v, 0]
        face_x[1, v * CY : (v + 1) * CY, :] = q_now[v, CX - 1]
    faces = face_copies(ix, iy, face_x, face_y, halo_x, halo_y, send, recv)
    for copy in faces:
        copy.start()
    packed = jnp.zeros((10 * CAP, NDEV), F32)
    for c in range(0, 2):
        packed = packed + donate(c, now_hi, now_lo, z_parts, w_xy, slots, onehot_b, ())
    for copy in first_a:
        copy.wait_recv()
    first_b = along_gy(0)
    for c in range(2, 4):
        packed = packed + donate(c, now_hi, now_lo, z_parts, w_xy, slots, onehot_b, ())
    sent[1, :, :, 0, :] = by_block(packed, 0)
    second_a = along_gx(1)
    hi, lo = two(flux_matrix(flux))
    km_hi[...] = hi
    km_lo[...] = lo
    for copy in faces:
        copy.wait()
    ends, rows = beyond(halo_x, halo_y)
    for x in range(CX):
        flux_x = flux_of(x, km_hi, km_lo, now_hi, now_lo, ends, rows)
        scale = 0.2 * jac[x]
        for v in range(V):
            part = slice(v * CY, (v + 1) * CY)
            start[x, part, :] = q_now[v, x] - scale * (flux_x[part] + (q_prev[v, x] - q_now[v, x]))
    for copy in second_a:
        copy.wait_recv()
    second_b = along_gy(1)
    for copy in first_b:
        copy.wait_recv()

    def spread(wave):
        rows = got[wave, :, :, 0, :].reshape(NDEV, 128)
        turned = rows.T
        for s in range(CAP):
            lanes = slice(s * NDEV, (s + 1) * NDEV)
            for v in range(V):
                hi, lo = two(jnp.broadcast_to(turned[v * CAP + s :][:1], (CY, NDEV)))
                parts[wave * 11 + v, :, lanes] = hi
                parts[wave * 11 + V + v, :, lanes] = lo
        return rows, turned

    rows, turned = spread(0)
    parts[10] = jnp.ones((CY, NDEV * CAP), BF16)
    for s in range(CAP):
        lanes = slice(s * NDEV, (s + 1) * NDEV)
        places[:, lanes] = jnp.broadcast_to(turned[5 * CAP + s :][:1], (CY, NDEV))
        column = rows[:, 6 * CAP + s : 6 * CAP + s + 1]
        at_z[lanes, :] = (iota((NDEV, CZ), 1).astype(F32) == column).astype(F32).astype(BF16)

    def landing(group, first, last):
        left = []
        for j in range(GROUP):
            mark = (iota((CY, 1), 0) + ((group * GROUP + j) * CY + 1)).astype(F32)
            here = (places[...] == mark).astype(F32).astype(BF16)
            left += [parts[i] * here for i in range(first, last)]
        return dot(jnp.concatenate(left, axis=0), at_z[...])

    def rows_of(landed, j, n, i):
        return landed[(j * n + i) * CY : (j * n + i + 1) * CY]

    for group in range(CX // GROUP):
        landed = landing(group, 0, 11)
        for j in range(GROUP):
            x = group * GROUP + j
            scale = 0.2 * jac[x]
            hits = rows_of(landed, j, 11, 10)
            fresh = []
            for v in range(V):
                part = slice(v * CY, (v + 1) * CY)
                q, qp = q_now[v, x], q_prev[v, x]
                target = rows_of(landed, j, 11, v) + rows_of(landed, j, 11, V + v)
                w = start[x, part, :] - scale * (2.0 * (hits * q - target))
                hi, lo = two(w)
                hi_out[x, part, :] = hi
                lo_out[x, part, :] = lo
                later[x, part, :] = w - scale * ((3.0 * w - 4.0 * q + qp) + 2.0 * (hits * w))
                fresh.append(w)
                if x in (0, CX - 1):
                    face2_x[0 if x == 0 else 1, part, :] = w
            lo_y, hi_y = y_faces(fresh)
            face2_y[0, x] = lo_y
            face2_y[1, x] = hi_y
    faces2 = face_copies(ix, iy, face2_x, face2_y, halo2_x, halo2_y, send2, recv2)
    for copy in faces2:
        copy.start()
    for copy in second_b:
        copy.wait_recv()
    spread(1)
    for group in range(CX // GROUP):
        landed = landing(group, 11, 21)
        for j in range(GROUP):
            x = group * GROUP + j
            scale = 0.4 * jac[x]
            for v in range(V):
                part = slice(v * CY, (v + 1) * CY)
                target = rows_of(landed, j, 10, v) + rows_of(landed, j, 10, V + v)
                later[x, part, :] = later[x, part, :] + scale * target
    for copy in first_a + first_b + second_a + second_b:
        copy.wait_send()
    for copy in faces2:
        copy.wait()


def second(hi, lo, later, jac, halo_x, halo_y, km_hi, km_lo, out):
    ends, rows = beyond(halo_x, halo_y)
    for x in range(CX):
        flux = flux_of(x, km_hi, km_lo, hi, lo, ends, rows)
        scale = 0.2 * jac[x]
        for v in range(V):
            part = slice(v * CY, (v + 1) * CY)
            out[v, x] = later[x, part, :] - scale * flux[part]


VM = pl.BlockSpec(memory_space=pltpu.VMEM)
SM = pl.BlockSpec(memory_space=pltpu.SMEM)
HB = pl.BlockSpec(memory_space=pltpu.HBM)
FACES = [((2, VY, CZ), F32), ((2, CX, 8, CZ), F32)]
PLANES = ((CX, VY, CZ), F32)
PARTS = [((CX, VY, CZ), BF16)] * 2
MATRIX = [((3 * VY, 256), BF16)] * 2


def shapes(entries):
    return [jax.ShapeDtypeStruct(*e) for e in entries]


def vmem(entries):
    return [pltpu.VMEM(*e) for e in entries]


def call_advance(count, flux, q_now, q_prev, jac, base, frac, dest, cell):
    ins = [pltpu.with_memory_space_constraint(a, pltpu.HBM) for a in (flux, q_now, q_prev, jac, base, frac, dest, cell)]
    dma = pltpu.SemaphoreType.DMA
    return pl.pallas_call(
        advance,
        out_shape=shapes([PLANES] + PARTS + FACES + MATRIX),
        in_specs=[SM] + [HB] * 8,
        out_specs=[VM] * 7,
        scratch_shapes=vmem([(a.shape, a.dtype) for a in ins])
        + vmem(PARTS * 2 + [PLANES, ((4, 3 * CZ, CHUNK), BF16), ((4, CX, CY, CHUNK), F32)])
        + vmem([((2, GX, GY, 1, 128), F32)] * 2 + [((2, GY, GX, 1, 128), F32)] + FACES * 3)
        + vmem([((21, CY, NDEV * CAP), BF16), ((CY, NDEV * CAP), F32), ((NDEV * CAP, CZ), BF16)])
        + [dma((8,))] + [dma((4,))] * 4 + [dma((2, GX - 1))] * 2 + [dma((2, GY - 1))] * 2,
        compiler_params=pltpu.CompilerParams(vmem_limit_bytes=LIMIT, collective_id=0, has_side_effects=True),
        name="advance",
    )(count, *ins)


def call_second(hi, lo, later, jac, halo_x, halo_y, km_hi, km_lo):
    return pl.pallas_call(
        second,
        out_shape=jax.ShapeDtypeStruct((V, CX, CY, CZ), F32),
        in_specs=[VM] * 8,
        out_specs=VM,
        compiler_params=pltpu.CompilerParams(vmem_limit_bytes=LIMIT),
        name="second",
    )(hi, lo, later, jac, halo_x, halo_y, km_hi, km_lo)


def body(q_now, q_prev, jacobian, flux_split, donor_base, donor_frac, fringe_dest, receptor_cell, fringe_count):
    later, hi, lo, halo_x, halo_y, km_hi, km_lo = call_advance(
        fringe_count, flux_split.transpose(0, 2, 1, 3), q_now, q_prev, jacobian, donor_base.reshape(1, ROWS),
        donor_frac, fringe_dest.reshape(1, ROWS), receptor_cell.reshape(1, ROWS),
    )
    return call_second(hi, lo, later, jacobian, halo_x, halo_y, km_hi, km_lo)


def solution(mesh):
    return jax.shard_map(
        body,
        mesh=mesh,
        in_specs=(
            P(None, "gx", "gy", None),
            P(None, "gx", "gy", None),
            P("gx", "gy", None),
            P(),
            P(("gx", "gy")),
            P(None, ("gx", "gy")),
            P(("gx", "gy"), None),
            P(("gx", "gy")),
            P(("gx", "gy")),
        ),
        out_specs=P(None, "gx", "gy", None),
        check_vma=False,
    )
```

```python
import jax
import jax.numpy as jnp
from jax import lax
from jax.experimental import pallas as pl
from jax.experimental.pallas import tpu as pltpu
from jax.sharding import PartitionSpec as P

MESH = pl.DeviceIdType.MESH
F32 = jnp.float32
BF16 = jnp.bfloat16
V, CX, CY, CZ = 5, 16, 16, 256
ROWS = 1024
NDEV = 128
CAP = 16
GX, GY = 8, 16
VY = V * CY
CHUNK = 256
GROUP = 4
LIMIT = 48 * 1024 * 1024


def iota(shape, dim):
    return lax.broadcasted_iota(jnp.int32, shape, dim)


def two(a):
    hi = a.astype(BF16)
    return hi, (a - hi.astype(F32)).astype(BF16)


def dot(a, b):
    return lax.dot_general(a, b, (((1,), (0,)), ((), ())), preferred_element_type=F32)


def dot_t(a, b):
    return lax.dot_general(a, b, (((1,), (1,)), ((), ())), preferred_element_type=F32)


def flux_matrix(flux):
    col = iota((1, 256), 1)
    block = (col >= 80).astype(jnp.int32) + (col >= 160).astype(jnp.int32) + (col >= 240).astype(jnp.int32)
    side = (col >= 248).astype(jnp.int32)
    var = jnp.where(block == 3, col - 240 - 8 * side, (col >> 4) - 5 * block)
    yc = jnp.where(block == 3, 17 * side - 1, col & 15)
    y = iota((CY, 256), 0)
    here = (yc == y).astype(F32)
    back = (yc == y - 1).astype(F32)
    fwd = (yc == y + 1).astype(F32)
    mid = (block == 1).astype(F32)
    near = ((block == 1) | (block == 3)).astype(F32)
    w_mid, w_back, w_fwd = here * mid, back * near, fwd * near
    w_left, w_right = here * (block == 0).astype(F32), here * (block == 2).astype(F32)
    mains, ups, downs = [], [], []
    for a in range(V):
        row = {}
        for d in range(3):
            for s in range(2):
                total = jnp.zeros((1, 256), F32)
                for b in range(V):
                    total = jnp.where(var == b, flux[d, a, s : s + 1, b : b + 1], total)
                row[d, s] = total
        centre = (row[0, 0] - row[0, 1]) + (row[1, 0] - row[1, 1]) + (row[2, 0] - row[2, 1])
        mains.append(
            centre * w_mid - row[1, 0] * w_back + row[1, 1] * w_fwd - row[0, 0] * w_left + row[0, 1] * w_right
        )
        ups.append(row[2, 1] * w_mid)
        downs.append(row[2, 0] * w_mid)
    return jnp.concatenate(mains + ups + downs, axis=0)


def beyond(halo_x, halo_y):
    ix, iy = lax.axis_index("gx"), lax.axis_index("gy")
    nx, ny = lax.axis_size("gx"), lax.axis_size("gy")
    keep_x = [jnp.where(ix > 0, 1.0, 0.0), jnp.where(ix < nx - 1, 1.0, 0.0)]
    keep_y = [jnp.where(iy > 0, 1.0, 0.0), jnp.where(iy < ny - 1, 1.0, 0.0)]
    ends = [two(halo_x[side] * keep_x[side]) for side in range(2)]
    pad = jnp.zeros((8 - V, CZ), F32)

    def row(x):
        tiles = []
        for side in range(2):
            both = [halo_y[side, h, pl.ds(x, V, stride=CX), :] for h in range(2)]
            tiles += [jnp.concatenate(both, axis=1) * keep_y[side], pad]
        return two(jnp.concatenate(tiles, axis=0))

    rows = [row(x) for x in range(CX)]
    return ends, rows


def flux_of(x, km_hi, km_lo, hi, lo, ends, rows):
    def tile(ref, part):
        left = ends[0][part] if x == 0 else ref[x - 1]
        right = ends[1][part] if x == CX - 1 else ref[x + 1]
        return jnp.concatenate([left, ref[x], right, rows[x][part]], axis=0)

    top, low = tile(hi, 0), tile(lo, 1)
    total = dot(km_hi[...], top) + dot(km_lo[...], top) + dot(km_hi[...], low)
    z = iota((VY, CZ), 1)
    fwd = jnp.where(z == CZ - 1, 0.0, pltpu.roll(total[VY : 2 * VY], CZ - 1, 1))
    back = jnp.where(z == 0, 0.0, pltpu.roll(total[2 * VY :], 1, 1))
    return total[:VY] + fwd - back


def face_copies(ix, iy, face_x, face_y, halo_x, halo_y, send, recv):
    copies = []
    for side in range(2):
        step = 2 * side - 1
        peer_x = lax.rem(ix + step + GX, GX)
        peer_y = lax.rem(iy + step + GY, GY)
        copies.append(
            pltpu.make_async_remote_copy(
                face_x.at[side], halo_x.at[1 - side], send.at[0], recv.at[0],
                device_id=(peer_x, iy), device_id_type=MESH,
            )
        )
        copies.append(
            pltpu.make_async_remote_copy(
                face_y.at[side], halo_y.at[1 - side], send.at[1], recv.at[1],
                device_id=(ix, peer_y), device_id_type=MESH,
            )
        )
    return copies


def arrived(ref, sem):
    pltpu.make_async_copy(ref, ref, sem).wait()


def ranks(onehot, onehot_b):
    before = (iota((CHUNK, CHUNK), 0) < iota((CHUNK, CHUNK), 1)).astype(F32).astype(BF16)
    ones = jnp.ones((CHUNK, CHUNK), BF16)
    carry = jnp.zeros((NDEV, CHUNK), F32)
    slots = []
    for c in range(ROWS // CHUNK):
        part = onehot_b[:, c * CHUNK : (c + 1) * CHUNK]
        rank = dot(part, before) + carry
        carry = carry + dot(part, ones)
        slots.append(jnp.sum(rank * onehot[:, c * CHUNK : (c + 1) * CHUNK], axis=0, keepdims=True))
    return slots


def hat(n, low, f):
    at = iota((n, CHUNK), 0)
    return jnp.where(at == low, 1.0 - f, jnp.where(at == low + 1, f, jnp.zeros_like(f)))


def stencils(base, frac, z_parts, w_xy):
    for c in range(ROWS // CHUNK):
        span = slice(c * CHUNK, (c + 1) * CHUNK)
        low = base[:, span]
        base_x = low // ((CZ - 1) * (CY - 1))
        rest = low - base_x * ((CZ - 1) * (CY - 1))
        base_y = rest // (CZ - 1)
        base_z = rest - base_y * (CZ - 1)
        fx, fy, fz = frac[0:1, span], frac[1:2, span], frac[2:3, span]
        hi, lo = two(hat(CZ, base_z, fz))
        z_parts[c, 0:CZ, :] = hi
        z_parts[c, CZ : 2 * CZ, :] = hi
        z_parts[c, 2 * CZ :, :] = lo
        w_x, w_y = hat(CX, base_x, fx), hat(CY, base_y, fy)
        for x in range(CX):
            w_xy[c, x] = w_x[x : x + 1] * w_y


def donate(c, hi, lo, z_parts, w_xy, slots, onehot_b, extra):
    top, rem = hi[...].reshape(CX * VY, CZ), lo[...].reshape(CX * VY, CZ)
    along = dot(jnp.concatenate([top, rem, top], axis=1), z_parts[c])
    at_slot = (iota((CAP, CHUNK), 0).astype(F32) == slots[c]).astype(F32)
    rows_hi, rows_lo = [], []
    for v in range(V):
        total = jnp.zeros((CY, CHUNK), F32)
        for x in range(CX):
            at = x * VY + v * CY
            total = total + along[at : at + CY] * w_xy[c, x]
        value = jnp.sum(total, axis=0, keepdims=True)
        first = value.astype(BF16).astype(F32)
        rows_hi.append((at_slot * first).astype(BF16))
        rows_lo.append((at_slot * (value - first)).astype(BF16))
    rows_hi += [(at_slot * part.astype(F32)).astype(BF16) for part in extra]
    return dot_t(jnp.concatenate(rows_hi + rows_lo, axis=0), onehot_b[:, c * CHUNK : (c + 1) * CHUNK])


def by_block(packed, extra):
    n, m = V * CAP, (V + extra) * CAP
    rows = [packed[:n] + packed[m:]] + ([packed[n:m]] if extra else []) + [jnp.zeros((128 - m, NDEV), F32)]
    return jnp.concatenate(rows, axis=0).T.reshape(GX, GY, 128)


def advance(count, flux_h, now_h, prev_h, jac_h, base_h, frac_h, dest_h, cell_h,
            later, hi_out, lo_out, halo2_x, halo2_y, km_hi, km_lo,
            flux, q_now, q_prev, jac, base, frac, dest, cell, now_hi, now_lo, prev_hi, prev_lo, start, z_parts, w_xy,
            sent, mid, got, face_x, face_y, halo_x, halo_y, face2_x, face2_y, parts, places, at_z,
            load, send, recv, send2, recv2, send_a, recv_a, send_b, recv_b):
    loads = [
        pltpu.make_async_copy(a, b, load.at[i])
        for i, (a, b) in enumerate(
            [(dest_h, dest), (base_h, base), (frac_h, frac), (flux_h, flux), (cell_h, cell), (prev_h, q_prev),
             (now_h, q_now), (jac_h, jac)]
        )
    ]
    for copy in loads:
        copy.start()
    ix, iy = lax.axis_index("gx"), lax.axis_index("gy")
    peers = [(lax.rem(ix + k, GX), iy) for k in range(1, GX)] + [(ix, lax.rem(iy + k, GY)) for k in range(1, GY)]
    barrier = pltpu.get_barrier_semaphore()
    for peer in peers:
        pl.semaphore_signal(barrier, inc=1, device_id=peer, device_id_type=MESH)

    def along_gx(wave):
        copies = []
        for k in range(1, GX):
            to = lax.rem(ix + k, GX)
            copies.append(
                pltpu.make_async_remote_copy(
                    sent.at[wave, to], mid.at[wave, ix], send_a.at[wave], recv_a.at[wave],
                    device_id=(to, iy), device_id_type=MESH,
                )
            )
        for copy in copies:
            copy.start()
        mid[wave, ix] = sent[wave, ix]

    def along_gy(wave):
        copies = []
        for k in range(1, GY):
            to = lax.rem(iy + k, GY)
            copies.append(
                pltpu.make_async_remote_copy(
                    mid.at[wave, :, to], got.at[wave, iy], send_b.at[wave], recv_b.at[wave],
                    device_id=(ix, to), device_id_type=MESH,
                )
            )
        for copy in copies:
            copy.start()
        got[wave, iy] = mid[wave, :, iy]

    for copy in loads[:5]:
        copy.wait()
    live = iota((1, ROWS), 1) < count[0]
    where_to = jnp.where(live, dest[...], NDEV)
    onehot = (iota((NDEV, ROWS), 0) == where_to).astype(F32)
    onehot_b = onehot.astype(BF16)
    slots = ranks(onehot, onehot_b)
    stencils(base, frac, z_parts, w_xy)
    hi, lo = two(flux_matrix(flux))
    km_hi[...] = hi
    km_lo[...] = lo
    loads[5].wait()
    for x in range(CX):
        for v in range(V):
            hi, lo = two(q_prev[v, x])
            prev_hi[x, v * CY : (v + 1) * CY, :] = hi
            prev_lo[x, v * CY : (v + 1) * CY, :] = lo
    packed = jnp.zeros((12 * CAP, NDEV), F32)
    for c in range(ROWS // CHUNK):
        cells = cell[:, c * CHUNK : (c + 1) * CHUNK]
        packed = packed + donate(
            c, prev_hi, prev_lo, z_parts, w_xy, slots, onehot_b, ((cells >> 8) + 1, cells & 255)
        )
    sent[0, :, :, 0, :] = by_block(packed, 2)

    pl.semaphore_wait(barrier, len(peers))
    along_gx(0)
    for copy in loads[6:]:
        copy.wait()
    for x in range(CX):
        for v in range(V):
            hi, lo = two(q_now[v, x])
            now_hi[x, v * CY : (v + 1) * CY, :] = hi
            now_lo[x, v * CY : (v + 1) * CY, :] = lo
    for v in range(V):
        for side, y in ((0, 0), (1, CY - 1)):
            for h in range(2):
                face_y[side, h, v * CX : (v + 1) * CX, :] = q_now[v, :, y, h * 128 : (h + 1) * 128]
        face_x[0, v * CY : (v + 1) * CY, :] = q_now[v, 0]
        face_x[1, v * CY : (v + 1) * CY, :] = q_now[v, CX - 1]
    faces = face_copies(ix, iy, face_x, face_y, halo_x, halo_y, send, recv)
    for copy in faces:
        copy.start()
    packed = jnp.zeros((10 * CAP, NDEV), F32)
    for c in range(0, 2):
        packed = packed + donate(c, now_hi, now_lo, z_parts, w_xy, slots, onehot_b, ())
    arrived(mid.at[0, pl.ds(0, GX - 1)], recv_a.at[0])
    along_gy(0)
    for c in range(2, 4):
        packed = packed + donate(c, now_hi, now_lo, z_parts, w_xy, slots, onehot_b, ())
    sent[1, :, :, 0, :] = by_block(packed, 0)
    along_gx(1)
    arrived(halo_x, recv.at[0])
    arrived(halo_y, recv.at[1])
    ends, rows = beyond(halo_x, halo_y)
    for x in range(CX):
        flux_x = flux_of(x, km_hi, km_lo, now_hi, now_lo, ends, rows)
        scale = 0.2 * jac[x]
        for v in range(V):
            part = slice(v * CY, (v + 1) * CY)
            start[x, part, :] = q_now[v, x] - scale * (flux_x[part] + (q_prev[v, x] - q_now[v, x]))
    arrived(mid.at[1, pl.ds(0, GX - 1)], recv_a.at[1])
    along_gy(1)
    arrived(got.at[0, pl.ds(0, GY - 1)], recv_b.at[0])

    def spread(wave):
        rows = got[wave, :, :, 0, :].reshape(NDEV, 128)
        turned = rows.T
        for s in range(CAP):
            lanes = slice(s * NDEV, (s + 1) * NDEV)
            for v in range(V):
                hi, lo = two(jnp.broadcast_to(turned[v * CAP + s :][:1], (CY, NDEV)))
                parts[wave * 11 + v, :, lanes] = hi
                parts[wave * 11 + V + v, :, lanes] = lo
        return rows, turned

    rows, turned = spread(0)
    parts[10] = jnp.ones((CY, NDEV * CAP), BF16)
    for s in range(CAP):
        lanes = slice(s * NDEV, (s + 1) * NDEV)
        places[:, lanes] = jnp.broadcast_to(turned[5 * CAP + s :][:1], (CY, NDEV))
        column = rows[:, 6 * CAP + s : 6 * CAP + s + 1]
        at_z[lanes, :] = (iota((NDEV, CZ), 1).astype(F32) == column).astype(F32).astype(BF16)

    def landing(group, first, last):
        left = []
        for j in range(GROUP):
            mark = (iota((CY, 1), 0) + ((group * GROUP + j) * CY + 1)).astype(F32)
            here = (places[...] == mark).astype(F32).astype(BF16)
            left += [parts[i] * here for i in range(first, last)]
        return dot(jnp.concatenate(left, axis=0), at_z[...])

    def rows_of(landed, j, n, i):
        return landed[(j * n + i) * CY : (j * n + i + 1) * CY]

    for group in range(CX // GROUP):
        landed = landing(group, 0, 11)
        for j in range(GROUP):
            x = group * GROUP + j
            scale = 0.2 * jac[x]
            hits = rows_of(landed, j, 11, 10)
            for v in range(V):
                part = slice(v * CY, (v + 1) * CY)
                q, qp = q_now[v, x], q_prev[v, x]
                target = rows_of(landed, j, 11, v) + rows_of(landed, j, 11, V + v)
                w = start[x, part, :] - scale * (2.0 * (hits * q - target))
                hi, lo = two(w)
                hi_out[x, part, :] = hi
                lo_out[x, part, :] = lo
                later[x, part, :] = w - scale * ((3.0 * w - 4.0 * q + qp) + 2.0 * (hits * w))
                for side, y in ((0, 0), (1, CY - 1)):
                    for h in range(2):
                        row = w[y : y + 1, h * 128 : (h + 1) * 128]
                        face2_y[side, h, v * CX + x : v * CX + x + 1, :] = row
                if x in (0, CX - 1):
                    face2_x[0 if x == 0 else 1, part, :] = w
    faces2 = face_copies(ix, iy, face2_x, face2_y, halo2_x, halo2_y, send2, recv2)
    for copy in faces2:
        copy.start()
    arrived(got.at[1, pl.ds(0, GY - 1)], recv_b.at[1])
    spread(1)
    for group in range(CX // GROUP):
        landed = landing(group, 11, 21)
        for j in range(GROUP):
            x = group * GROUP + j
            scale = 0.4 * jac[x]
            for v in range(V):
                part = slice(v * CY, (v + 1) * CY)
                target = rows_of(landed, j, 10, v) + rows_of(landed, j, 10, V + v)
                later[x, part, :] = later[x, part, :] + scale * target
    for wave in range(2):
        arrived(sent.at[wave, pl.ds(0, GX - 1)], send_a.at[wave])
        arrived(got.at[wave, pl.ds(0, GY - 1)], send_b.at[wave])
    arrived(face_x, send.at[0])
    arrived(face_y, send.at[1])
    arrived(face2_x, send2.at[0])
    arrived(face2_y, send2.at[1])
    arrived(halo2_x, recv2.at[0])
    arrived(halo2_y, recv2.at[1])


def second(hi, lo, later, jac, halo_x, halo_y, km_hi, km_lo, out, plane, store):
    ends, rows = beyond(halo_x, halo_y)
    for x in range(CX):
        flux = flux_of(x, km_hi, km_lo, hi, lo, ends, rows)
        scale = 0.2 * jac[x]
        for v in range(V):
            part = slice(v * CY, (v + 1) * CY)
            plane[x, v] = later[x, part, :] - scale * flux[part]
        pltpu.make_async_copy(plane.at[x], out.at[:, x], store.at[x]).start()
    for x in range(CX):
        pltpu.make_async_copy(plane.at[x], out.at[:, x], store.at[x]).wait()


VM = pl.BlockSpec(memory_space=pltpu.VMEM)
SM = pl.BlockSpec(memory_space=pltpu.SMEM)
HB = pl.BlockSpec(memory_space=pltpu.HBM)
FACES = [((2, VY, CZ), F32), ((2, 2, VY, 128), F32)]
PLANES = ((CX, VY, CZ), F32)
PARTS = [((CX, VY, CZ), BF16)] * 2
MATRIX = [((3 * VY, 256), BF16)] * 2


def shapes(entries):
    return [jax.ShapeDtypeStruct(*e) for e in entries]


def vmem(entries):
    return [pltpu.VMEM(*e) for e in entries]


def call_advance(count, flux, q_now, q_prev, jac, base, frac, dest, cell):
    ins = [pltpu.with_memory_space_constraint(a, pltpu.HBM) for a in (flux, q_now, q_prev, jac, base, frac, dest, cell)]
    dma = pltpu.SemaphoreType.DMA
    return pl.pallas_call(
        advance,
        out_shape=shapes([PLANES] + PARTS + FACES + MATRIX),
        in_specs=[SM] + [HB] * 8,
        out_specs=[VM] * 7,
        scratch_shapes=vmem([(a.shape, a.dtype) for a in ins])
        + vmem(PARTS * 2 + [PLANES, ((4, 3 * CZ, CHUNK), BF16), ((4, CX, CY, CHUNK), F32)])
        + vmem([((2, GX, GY, 1, 128), F32)] * 2 + [((2, GY, GX, 1, 128), F32)] + FACES * 3)
        + vmem([((21, CY, NDEV * CAP), BF16), ((CY, NDEV * CAP), F32), ((NDEV * CAP, CZ), BF16)])
        + [dma((8,))] + [dma((2,))] * 8,
        compiler_params=pltpu.CompilerParams(vmem_limit_bytes=LIMIT, collective_id=0, has_side_effects=True),
        name="advance",
    )(count, *ins)


def call_second(hi, lo, later, jac, halo_x, halo_y, km_hi, km_lo):
    return pl.pallas_call(
        second,
        out_shape=jax.ShapeDtypeStruct((V, CX, CY, CZ), F32),
        in_specs=[VM] * 8,
        out_specs=HB,
        scratch_shapes=[pltpu.VMEM((CX, V, CY, CZ), F32), pltpu.SemaphoreType.DMA((CX,))],
        compiler_params=pltpu.CompilerParams(vmem_limit_bytes=LIMIT),
        name="second",
    )(hi, lo, later, jac, halo_x, halo_y, km_hi, km_lo)


def body(q_now, q_prev, jacobian, flux_split, donor_base, donor_frac, fringe_dest, receptor_cell, fringe_count):
    later, hi, lo, halo_x, halo_y, km_hi, km_lo = call_advance(
        fringe_count, flux_split.transpose(0, 2, 1, 3), q_now, q_prev, jacobian, donor_base.reshape(1, ROWS),
        donor_frac, fringe_dest.reshape(1, ROWS), receptor_cell.reshape(1, ROWS),
    )
    return call_second(hi, lo, later, jacobian, halo_x, halo_y, km_hi, km_lo)


def solution(mesh):
    return jax.shard_map(
        body,
        mesh=mesh,
        in_specs=(
            P(None, "gx", "gy", None),
            P(None, "gx", "gy", None),
            P("gx", "gy", None),
            P(),
            P(("gx", "gy")),
            P(None, ("gx", "gy")),
            P(("gx", "gy"), None),
            P(("gx", "gy")),
            P(("gx", "gy")),
        ),
        out_specs=P(None, "gx", "gy", None),
        check_vma=False,
    )
```

```python
import jax
import jax.numpy as jnp
from jax import lax
from jax.experimental import pallas as pl
from jax.experimental.pallas import tpu as pltpu
from jax.sharding import PartitionSpec as P

MESH = pl.DeviceIdType.MESH
F32 = jnp.float32
BF16 = jnp.bfloat16
V, CX, CY, CZ = 5, 16, 16, 256
ROWS = 1024
NDEV = 128
CAP = 16
GX, GY = 8, 16
VY = V * CY
CHUNK = 256
GROUP = 4
HALF = CX // 2
LIMIT = 48 * 1024 * 1024


def iota(shape, dim):
    return lax.broadcasted_iota(jnp.int32, shape, dim)


def two(a):
    hi = a.astype(BF16)
    return hi, (a - hi.astype(F32)).astype(BF16)


def dot(a, b):
    return lax.dot_general(a, b, (((1,), (0,)), ((), ())), preferred_element_type=F32)


def dot_t(a, b):
    return lax.dot_general(a, b, (((1,), (1,)), ((), ())), preferred_element_type=F32)


def flux_matrix(flux):
    col = iota((1, 256), 1)
    block = (col >= 80).astype(jnp.int32) + (col >= 160).astype(jnp.int32) + (col >= 240).astype(jnp.int32)
    side = (col >= 248).astype(jnp.int32)
    var = jnp.where(block == 3, col - 240 - 8 * side, (col >> 4) - 5 * block)
    yc = jnp.where(block == 3, 17 * side - 1, col & 15)
    y = iota((CY, 256), 0)
    here = (yc == y).astype(F32)
    back = (yc == y - 1).astype(F32)
    fwd = (yc == y + 1).astype(F32)
    mid = (block == 1).astype(F32)
    near = ((block == 1) | (block == 3)).astype(F32)
    w_mid, w_back, w_fwd = here * mid, back * near, fwd * near
    w_any = here * (block < 3).astype(F32)
    w_left, w_right = here * (block == 0).astype(F32), here * (block == 2).astype(F32)
    mains, ups, downs = [], [], []
    for a in range(V):
        row = {}
        for d in range(3):
            for s in range(2):
                total = jnp.zeros((1, 256), F32)
                for b in range(V):
                    total = jnp.where(var == b, flux[d, a, s : s + 1, b : b + 1], total)
                row[d, s] = total
        centre = (row[0, 0] - row[0, 1]) + (row[1, 0] - row[1, 1]) + (row[2, 0] - row[2, 1])
        mains.append(
            centre * w_mid - row[1, 0] * w_back + row[1, 1] * w_fwd - row[0, 0] * w_left + row[0, 1] * w_right
        )
        ups.append(row[2, 1] * w_any)
        downs.append(row[2, 0] * w_any)
    hi, lo = two(jnp.concatenate(mains, axis=0))
    along = jnp.concatenate(ups + downs, axis=0)
    top = along.astype(BF16).astype(F32)
    return jnp.concatenate([hi, lo], axis=0), jnp.where(block == 1, along - top, top).astype(BF16)


def beyond(halo_x, halo_y):
    ix, iy = lax.axis_index("gx"), lax.axis_index("gy")
    nx, ny = lax.axis_size("gx"), lax.axis_size("gy")
    keep_x = [jnp.where(ix > 0, 1.0, 0.0), jnp.where(ix < nx - 1, 1.0, 0.0)]
    keep_y = [jnp.where(iy > 0, 1.0, 0.0), jnp.where(iy < ny - 1, 1.0, 0.0)]
    ends = [two(halo_x[side] * keep_x[side]) for side in range(2)]
    pad = jnp.zeros((8 - V, CZ), F32)

    def row(x):
        tiles = []
        for side in range(2):
            both = [halo_y[x // HALF, side, h, pl.ds(x % HALF, V, stride=HALF), :] for h in range(2)]
            tiles += [jnp.concatenate(both, axis=1) * keep_y[side], pad]
        return two(jnp.concatenate(tiles, axis=0))

    rows = [row(x) for x in range(CX)]
    return ends, rows


def flux_of(x, km_xy, km_z, hi, lo, ends, rows):
    def tile(ref, part):
        left = ends[0][part] if x == 0 else ref[x - 1]
        right = ends[1][part] if x == CX - 1 else ref[x + 1]
        return jnp.concatenate([left, ref[x], right, rows[x][part]], axis=0)

    both = dot(km_xy[...], tile(hi, 0))
    total = both[:VY] + both[VY:] + dot(km_xy[:VY], tile(lo, 1))
    along = dot(km_z[:, : 3 * VY], jnp.concatenate([hi[x], hi[x], lo[x]], axis=0))
    z = iota((VY, CZ), 1)
    fwd = jnp.where(z == CZ - 1, 0.0, pltpu.roll(along[:VY], CZ - 1, 1))
    back = jnp.where(z == 0, 0.0, pltpu.roll(along[VY:], 1, 1))
    return total + fwd - back


def x_copies(ix, iy, face_x, halo_x, send, recv):
    copies = []
    for side in range(2):
        peer = lax.rem(ix + 2 * side - 1 + GX, GX)
        copies.append(
            pltpu.make_async_remote_copy(
                face_x.at[side], halo_x.at[1 - side], send, recv, device_id=(peer, iy), device_id_type=MESH
            )
        )
    return copies


def y_copies(ix, iy, face_y, halo_y, piece, send, recv):
    copies = []
    for side in range(2):
        peer = lax.rem(iy + 2 * side - 1 + GY, GY)
        copies.append(
            pltpu.make_async_remote_copy(
                face_y.at[piece, side], halo_y.at[piece, 1 - side], send, recv,
                device_id=(ix, peer), device_id_type=MESH,
            )
        )
    return copies


def arrived(ref, sem):
    pltpu.make_async_copy(ref, ref, sem).wait()


def ranks(onehot, onehot_b):
    before = (iota((CHUNK, CHUNK), 0) < iota((CHUNK, CHUNK), 1)).astype(F32).astype(BF16)
    ones = jnp.ones((CHUNK, CHUNK), BF16)
    carry = jnp.zeros((NDEV, CHUNK), F32)
    slots = []
    for c in range(ROWS // CHUNK):
        part = onehot_b[:, c * CHUNK : (c + 1) * CHUNK]
        rank = dot(part, before) + carry
        carry = carry + dot(part, ones)
        slots.append(jnp.sum(rank * onehot[:, c * CHUNK : (c + 1) * CHUNK], axis=0, keepdims=True))
    return slots


def hat(n, low, f):
    at = iota((n, CHUNK), 0)
    return jnp.where(at == low, 1.0 - f, jnp.where(at == low + 1, f, jnp.zeros_like(f)))


def stencils(base, frac, z_parts, w_xy):
    for c in range(ROWS // CHUNK):
        span = slice(c * CHUNK, (c + 1) * CHUNK)
        low = base[:, span]
        base_x = low // ((CZ - 1) * (CY - 1))
        rest = low - base_x * ((CZ - 1) * (CY - 1))
        base_y = rest // (CZ - 1)
        base_z = rest - base_y * (CZ - 1)
        fx, fy, fz = frac[0:1, span], frac[1:2, span], frac[2:3, span]
        hi, lo = two(hat(CZ, base_z, fz))
        z_parts[c, 0:CZ, :] = hi
        z_parts[c, CZ : 2 * CZ, :] = hi
        z_parts[c, 2 * CZ :, :] = lo
        w_x, w_y = hat(CX, base_x, fx), hat(CY, base_y, fy)
        for x in range(CX):
            w_xy[c, x] = w_x[x : x + 1] * w_y


def donate(c, hi, lo, z_parts, w_xy, slots, onehot_b, extra):
    top, rem = hi[...].reshape(CX * VY, CZ), lo[...].reshape(CX * VY, CZ)
    along = dot(jnp.concatenate([top, rem, top], axis=1), z_parts[c])
    at_slot = (iota((CAP, CHUNK), 0).astype(F32) == slots[c]).astype(F32)
    rows_hi, rows_lo = [], []
    for v in range(V):
        total = jnp.zeros((CY, CHUNK), F32)
        for x in range(CX):
            at = x * VY + v * CY
            total = total + along[at : at + CY] * w_xy[c, x]
        value = jnp.sum(total, axis=0, keepdims=True)
        first = value.astype(BF16).astype(F32)
        rows_hi.append((at_slot * first).astype(BF16))
        rows_lo.append((at_slot * (value - first)).astype(BF16))
    rows_hi += [(at_slot * part.astype(F32)).astype(BF16) for part in extra]
    return dot_t(jnp.concatenate(rows_hi + rows_lo, axis=0), onehot_b[:, c * CHUNK : (c + 1) * CHUNK])


def by_block(packed, extra):
    n, m = V * CAP, (V + extra) * CAP
    rows = [packed[:n] + packed[m:]] + ([packed[n:m]] if extra else []) + [jnp.zeros((128 - m, NDEV), F32)]
    return jnp.concatenate(rows, axis=0).T.reshape(GX, GY, 128)


def advance(count, flux_h, now_h, prev_h, jac_h, base_h, frac_h, dest_h, cell_h,
            later, hi_out, lo_out, halo2_x, halo2_y, km_xy, km_z,
            flux, q_now, q_prev, jac, base, frac, dest, cell, now_hi, now_lo, prev_hi, prev_lo, start, z_parts, w_xy,
            sent, mid, got, face_x, face_y, halo_x, halo_y, face2_x, face2_y, parts, places, at_z,
            load, send, recv, send2, recv2, send_a, recv_a, send_b, recv_b):
    loads = [
        pltpu.make_async_copy(a, b, load.at[i])
        for i, (a, b) in enumerate(
            [(dest_h, dest), (base_h, base), (frac_h, frac), (flux_h, flux), (cell_h, cell), (now_h, q_now),
             (jac_h, jac)]
        )
    ]
    for copy in loads[:5]:
        copy.start()
    for v in range(V):
        pltpu.make_async_copy(prev_h.at[v], q_prev.at[v], load.at[7]).start()
    ix, iy = lax.axis_index("gx"), lax.axis_index("gy")
    peers = [(lax.rem(ix + k, GX), iy) for k in range(1, GX)] + [(ix, lax.rem(iy + k, GY)) for k in range(1, GY)]
    barrier = pltpu.get_barrier_semaphore()
    for peer in peers:
        pl.semaphore_signal(barrier, inc=1, device_id=peer, device_id_type=MESH)

    def along_gx(wave):
        copies = []
        for k in range(1, GX):
            to = lax.rem(ix + k, GX)
            copies.append(
                pltpu.make_async_remote_copy(
                    sent.at[wave, to], mid.at[wave, ix], send_a.at[wave], recv_a.at[wave],
                    device_id=(to, iy), device_id_type=MESH,
                )
            )
        for copy in copies:
            copy.start()
        mid[wave, ix] = sent[wave, ix]

    def along_gy(wave):
        copies = []
        for k in range(1, GY):
            to = lax.rem(iy + k, GY)
            copies.append(
                pltpu.make_async_remote_copy(
                    mid.at[wave, :, to], got.at[wave, iy], send_b.at[wave], recv_b.at[wave],
                    device_id=(ix, to), device_id_type=MESH,
                )
            )
        for copy in copies:
            copy.start()
        got[wave, iy] = mid[wave, :, iy]

    for copy in loads[:5]:
        copy.wait()
    live = iota((1, ROWS), 1) < count[0]
    where_to = jnp.where(live, dest[...], NDEV)
    onehot = (iota((NDEV, ROWS), 0) == where_to).astype(F32)
    onehot_b = onehot.astype(BF16)
    slots = ranks(onehot, onehot_b)
    stencils(base, frac, z_parts, w_xy)
    mat_xy, mat_z = flux_matrix(flux)
    km_xy[...] = mat_xy
    km_z[...] = mat_z
    arrived(q_prev, load.at[7])
    for copy in loads[5:]:
        copy.start()
    for x in range(CX):
        for v in range(V):
            hi, lo = two(q_prev[v, x])
            prev_hi[x, v * CY : (v + 1) * CY, :] = hi
            prev_lo[x, v * CY : (v + 1) * CY, :] = lo
    packed = jnp.zeros((12 * CAP, NDEV), F32)
    for c in range(ROWS // CHUNK):
        cells = cell[:, c * CHUNK : (c + 1) * CHUNK]
        packed = packed + donate(
            c, prev_hi, prev_lo, z_parts, w_xy, slots, onehot_b, ((cells >> 8) + 1, cells & 255)
        )
    sent[0, :, :, 0, :] = by_block(packed, 2)

    pl.semaphore_wait(barrier, len(peers))
    along_gx(0)
    for copy in loads[5:]:
        copy.wait()
    for x in range(CX):
        for v in range(V):
            hi, lo = two(q_now[v, x])
            now_hi[x, v * CY : (v + 1) * CY, :] = hi
            now_lo[x, v * CY : (v + 1) * CY, :] = lo
    for v in range(V):
        for side, y in ((0, 0), (1, CY - 1)):
            for h in range(2):
                for p in range(2):
                    face_y[p, side, h, v * HALF : (v + 1) * HALF, :] = q_now[
                        v, p * HALF : (p + 1) * HALF, y, h * 128 : (h + 1) * 128
                    ]
        face_x[0, v * CY : (v + 1) * CY, :] = q_now[v, 0]
        face_x[1, v * CY : (v + 1) * CY, :] = q_now[v, CX - 1]
    for copy in x_copies(ix, iy, face_x, halo_x, send.at[0], recv.at[0]):
        copy.start()
    for p in range(2):
        for copy in y_copies(ix, iy, face_y, halo_y, p, send.at[1], recv.at[1]):
            copy.start()
    packed = jnp.zeros((10 * CAP, NDEV), F32)
    for c in range(0, 2):
        packed = packed + donate(c, now_hi, now_lo, z_parts, w_xy, slots, onehot_b, ())
    arrived(mid.at[0, pl.ds(0, GX - 1)], recv_a.at[0])
    along_gy(0)
    for c in range(2, 4):
        packed = packed + donate(c, now_hi, now_lo, z_parts, w_xy, slots, onehot_b, ())
    sent[1, :, :, 0, :] = by_block(packed, 0)
    along_gx(1)
    arrived(halo_x, recv.at[0])
    arrived(halo_y, recv.at[1])
    ends, rows = beyond(halo_x, halo_y)
    for x in range(CX):
        flux_x = flux_of(x, km_xy, km_z, now_hi, now_lo, ends, rows)
        scale = 0.2 * jac[x]
        for v in range(V):
            part = slice(v * CY, (v + 1) * CY)
            start[x, part, :] = q_now[v, x] - scale * (flux_x[part] + (q_prev[v, x] - q_now[v, x]))
    arrived(got.at[0, pl.ds(0, GY - 1)], recv_b.at[0])

    def spread(wave):
        rows = got[wave, :, :, 0, :].reshape(NDEV, 128)
        turned = rows.T
        for s in range(CAP):
            lanes = slice(s * NDEV, (s + 1) * NDEV)
            for v in range(V):
                hi, lo = two(jnp.broadcast_to(turned[v * CAP + s :][:1], (CY, NDEV)))
                parts[wave * 11 + v, :, lanes] = hi
                parts[wave * 11 + V + v, :, lanes] = lo
        return rows, turned

    rows, turned = spread(0)
    parts[10] = jnp.ones((CY, NDEV * CAP), BF16)
    for s in range(CAP):
        lanes = slice(s * NDEV, (s + 1) * NDEV)
        places[:, lanes] = jnp.broadcast_to(turned[5 * CAP + s :][:1], (CY, NDEV))
        column = rows[:, 6 * CAP + s : 6 * CAP + s + 1]
        at_z[lanes, :] = (iota((NDEV, CZ), 1).astype(F32) == column).astype(F32).astype(BF16)

    def landing(group, first, last):
        left = []
        for j in range(GROUP):
            mark = (iota((CY, 1), 0) + ((group * GROUP + j) * CY + 1)).astype(F32)
            here = (places[...] == mark).astype(F32).astype(BF16)
            left += [parts[i] * here for i in range(first, last)]
        return dot(jnp.concatenate(left, axis=0), at_z[...])

    def rows_of(landed, j, n, i):
        return landed[(j * n + i) * CY : (j * n + i + 1) * CY]

    for group in range(CX // GROUP):
        landed = landing(group, 0, 11)
        for j in range(GROUP):
            x = group * GROUP + j
            scale = 0.2 * jac[x]
            hits = rows_of(landed, j, 11, 10)
            for v in range(V):
                part = slice(v * CY, (v + 1) * CY)
                q, qp = q_now[v, x], q_prev[v, x]
                target = rows_of(landed, j, 11, v) + rows_of(landed, j, 11, V + v)
                w = start[x, part, :] - scale * (2.0 * (hits * q - target))
                hi, lo = two(w)
                hi_out[x, part, :] = hi
                lo_out[x, part, :] = lo
                later[x, part, :] = w - scale * ((3.0 * w - 4.0 * q + qp) + 2.0 * (hits * w))
                for side, y in ((0, 0), (1, CY - 1)):
                    for h in range(2):
                        row = w[y : y + 1, h * 128 : (h + 1) * 128]
                        at = v * HALF + x % HALF
                        face2_y[x // HALF, side, h, at : at + 1, :] = row
                if x in (0, CX - 1):
                    face2_x[0 if x == 0 else 1, part, :] = w
        if group == 0:
            arrived(mid.at[1, pl.ds(0, GX - 1)], recv_a.at[1])
            along_gy(1)
        if group % 2 == 1:
            p = group // 2
            for copy in y_copies(ix, iy, face2_y, halo2_y, p, send2.at[1 + p], recv2.at[1 + p]):
                copy.start()
    for copy in x_copies(ix, iy, face2_x, halo2_x, send2.at[0], recv2.at[0]):
        copy.start()
    arrived(got.at[1, pl.ds(0, GY - 1)], recv_b.at[1])
    spread(1)
    for group in range(CX // GROUP):
        landed = landing(group, 11, 21)
        for j in range(GROUP):
            x = group * GROUP + j
            scale = 0.4 * jac[x]
            for v in range(V):
                part = slice(v * CY, (v + 1) * CY)
                target = rows_of(landed, j, 10, v) + rows_of(landed, j, 10, V + v)
                later[x, part, :] = later[x, part, :] + scale * target
    for wave in range(2):
        arrived(sent.at[wave, pl.ds(0, GX - 1)], send_a.at[wave])
        arrived(got.at[wave, pl.ds(0, GY - 1)], send_b.at[wave])
    arrived(face_x, send.at[0])
    arrived(face_y, send.at[1])
    arrived(face2_x, send2.at[0])
    for p in range(2):
        arrived(face2_y.at[p], send2.at[1 + p])
        arrived(halo2_y.at[p], recv2.at[1 + p])
    arrived(halo2_x, recv2.at[0])


def second(hi, lo, later, jac, halo_x, halo_y, km_xy, km_z, out, plane, store):
    ends, rows = beyond(halo_x, halo_y)
    for x in range(CX):
        flux = flux_of(x, km_xy, km_z, hi, lo, ends, rows)
        scale = 0.2 * jac[x]
        for v in range(V):
            part = slice(v * CY, (v + 1) * CY)
            plane[x, v] = later[x, part, :] - scale * flux[part]
        pltpu.make_async_copy(plane.at[x], out.at[:, x], store.at[x]).start()
    for x in range(CX):
        pltpu.make_async_copy(plane.at[x], out.at[:, x], store.at[x]).wait()


VM = pl.BlockSpec(memory_space=pltpu.VMEM)
SM = pl.BlockSpec(memory_space=pltpu.SMEM)
HB = pl.BlockSpec(memory_space=pltpu.HBM)
FACES = [((2, VY, CZ), F32), ((2, 2, 2, V * HALF, 128), F32)]
PLANES = ((CX, VY, CZ), F32)
PARTS = [((CX, VY, CZ), BF16)] * 2
MATRIX = [((2 * VY, 256), BF16)] * 2


def shapes(entries):
    return [jax.ShapeDtypeStruct(*e) for e in entries]


def vmem(entries):
    return [pltpu.VMEM(*e) for e in entries]


def call_advance(count, flux, q_now, q_prev, jac, base, frac, dest, cell):
    ins = [pltpu.with_memory_space_constraint(a, pltpu.HBM) for a in (flux, q_now, q_prev, jac, base, frac, dest, cell)]
    dma = pltpu.SemaphoreType.DMA
    return pl.pallas_call(
        advance,
        out_shape=shapes([PLANES] + PARTS + FACES + MATRIX),
        in_specs=[SM] + [HB] * 8,
        out_specs=[VM] * 7,
        scratch_shapes=vmem([(a.shape, a.dtype) for a in ins])
        + vmem(PARTS * 2 + [PLANES, ((4, 3 * CZ, CHUNK), BF16), ((4, CX, CY, CHUNK), F32)])
        + vmem([((2, GX, GY, 1, 128), F32)] * 2 + [((2, GY, GX, 1, 128), F32)] + FACES * 3)
        + vmem([((21, CY, NDEV * CAP), BF16), ((CY, NDEV * CAP), F32), ((NDEV * CAP, CZ), BF16)])
        + [dma((8,))] + [dma((2,))] * 2 + [dma((3,))] * 2 + [dma((2,))] * 4,
        compiler_params=pltpu.CompilerParams(vmem_limit_bytes=LIMIT, collective_id=0, has_side_effects=True),
        name="advance",
    )(count, *ins)


def call_second(hi, lo, later, jac, halo_x, halo_y, km_xy, km_z):
    return pl.pallas_call(
        second,
        out_shape=jax.ShapeDtypeStruct((V, CX, CY, CZ), F32),
        in_specs=[VM] * 8,
        out_specs=HB,
        scratch_shapes=[pltpu.VMEM((CX, V, CY, CZ), F32), pltpu.SemaphoreType.DMA((CX,))],
        compiler_params=pltpu.CompilerParams(vmem_limit_bytes=LIMIT),
        name="second",
    )(hi, lo, later, jac, halo_x, halo_y, km_xy, km_z)


def body(q_now, q_prev, jacobian, flux_split, donor_base, donor_frac, fringe_dest, receptor_cell, fringe_count):
    later, hi, lo, halo_x, halo_y, km_xy, km_z = call_advance(
        fringe_count, flux_split.transpose(0, 2, 1, 3), q_now, q_prev, jacobian, donor_base.reshape(1, ROWS),
        donor_frac, fringe_dest.reshape(1, ROWS), receptor_cell.reshape(1, ROWS),
    )
    return call_second(hi, lo, later, jacobian, halo_x, halo_y, km_xy, km_z)


def solution(mesh):
    return jax.shard_map(
        body,
        mesh=mesh,
        in_specs=(
            P(None, "gx", "gy", None),
            P(None, "gx", "gy", None),
            P("gx", "gy", None),
            P(),
            P(("gx", "gy")),
            P(None, ("gx", "gy")),
            P(("gx", "gy"), None),
            P(("gx", "gy")),
            P(("gx", "gy")),
        ),
        out_specs=P(None, "gx", "gy", None),
        check_vma=False,
    )
```

```python
import jax
import jax.numpy as jnp
from jax import lax
from jax.experimental import pallas as pl
from jax.experimental.pallas import tpu as pltpu
from jax.sharding import PartitionSpec as P

MESH = pl.DeviceIdType.MESH
F32 = jnp.float32
BF16 = jnp.bfloat16
V, CX, CY, CZ = 5, 16, 16, 256
ROWS = 1024
NDEV = 128
CAP = 16
GX, GY = 8, 16
VY = V * CY
CHUNK = 256
GROUP = 4
HALF = CX // 2
LIMIT = 48 * 1024 * 1024


def iota(shape, dim):
    return lax.broadcasted_iota(jnp.int32, shape, dim)


def two(a):
    hi = a.astype(BF16)
    return hi, (a - hi.astype(F32)).astype(BF16)


def dot(a, b):
    return lax.dot_general(a, b, (((1,), (0,)), ((), ())), preferred_element_type=F32)


def dot_t(a, b):
    return lax.dot_general(a, b, (((1,), (1,)), ((), ())), preferred_element_type=F32)


def flux_matrix(flux):
    col = iota((1, 256), 1)
    block = (col >= 80).astype(jnp.int32) + (col >= 160).astype(jnp.int32) + (col >= 240).astype(jnp.int32)
    side = (col >= 248).astype(jnp.int32)
    var = jnp.where(block == 3, col - 240 - 8 * side, (col >> 4) - 5 * block)
    yc = jnp.where(block == 3, 17 * side - 1, col & 15)
    y = iota((CY, 256), 0)
    here = (yc == y).astype(F32)
    back = (yc == y - 1).astype(F32)
    fwd = (yc == y + 1).astype(F32)
    mid = (block == 1).astype(F32)
    near = ((block == 1) | (block == 3)).astype(F32)
    w_mid, w_back, w_fwd = here * mid, back * near, fwd * near
    w_any = here * (block < 3).astype(F32)
    w_left, w_right = here * (block == 0).astype(F32), here * (block == 2).astype(F32)
    mains, ups, downs = [], [], []
    for a in range(V):
        row = {}
        for d in range(3):
            for s in range(2):
                total = jnp.zeros((1, 256), F32)
                for b in range(V):
                    total = jnp.where(var == b, flux[d, a, s : s + 1, b : b + 1], total)
                row[d, s] = total
        centre = (row[0, 0] - row[0, 1]) + (row[1, 0] - row[1, 1]) + (row[2, 0] - row[2, 1])
        mains.append(
            centre * w_mid - row[1, 0] * w_back + row[1, 1] * w_fwd - row[0, 0] * w_left + row[0, 1] * w_right
        )
        ups.append(row[2, 1] * w_any)
        downs.append(row[2, 0] * w_any)
    hi, lo = two(jnp.concatenate(mains, axis=0))
    along = jnp.concatenate(ups + downs, axis=0)
    top = along.astype(BF16).astype(F32)
    return jnp.concatenate([hi, lo], axis=0), jnp.where(block == 1, along - top, top).astype(BF16)


def beyond(halo_x, halo_y):
    ix, iy = lax.axis_index("gx"), lax.axis_index("gy")
    nx, ny = lax.axis_size("gx"), lax.axis_size("gy")
    keep_x = [jnp.where(ix > 0, 1.0, 0.0), jnp.where(ix < nx - 1, 1.0, 0.0)]
    keep_y = [jnp.where(iy > 0, 1.0, 0.0), jnp.where(iy < ny - 1, 1.0, 0.0)]
    ends = [two(halo_x[side] * keep_x[side]) for side in range(2)]
    pad = jnp.zeros((8 - V, CZ), F32)

    def row(x):
        tiles = []
        for side in range(2):
            both = [halo_y[x // HALF, side, h, pl.ds(x % HALF, V, stride=HALF), :] for h in range(2)]
            tiles += [jnp.concatenate(both, axis=1) * keep_y[side], pad]
        return two(jnp.concatenate(tiles, axis=0))

    rows = [row(x) for x in range(CX)]
    return ends, rows


def flux_of(x, km_xy, km_z, hi, lo, ends, rows):
    def tile(ref, part):
        left = ends[0][part] if x == 0 else ref[x - 1]
        right = ends[1][part] if x == CX - 1 else ref[x + 1]
        return jnp.concatenate([left, ref[x], right, rows[x][part]], axis=0)

    both = dot(km_xy[...], tile(hi, 0))
    total = both[:VY] + both[VY:] + dot(km_xy[:VY], tile(lo, 1))
    along = dot(km_z[:, : 3 * VY], jnp.concatenate([hi[x], hi[x], lo[x]], axis=0))
    z = iota((VY, CZ), 1)
    fwd = jnp.where(z == CZ - 1, 0.0, pltpu.roll(along[:VY], CZ - 1, 1))
    back = jnp.where(z == 0, 0.0, pltpu.roll(along[VY:], 1, 1))
    return total + fwd - back


def x_copies(ix, iy, face_x, halo_x, send, recv):
    copies = []
    for side in range(2):
        peer = lax.rem(ix + 2 * side - 1 + GX, GX)
        copies.append(
            pltpu.make_async_remote_copy(
                face_x.at[side], halo_x.at[1 - side], send, recv, device_id=(peer, iy), device_id_type=MESH
            )
        )
    return copies


def y_copies(ix, iy, face_y, halo_y, piece, send, recv):
    copies = []
    for side in range(2):
        peer = lax.rem(iy + 2 * side - 1 + GY, GY)
        copies.append(
            pltpu.make_async_remote_copy(
                face_y.at[piece, side], halo_y.at[piece, 1 - side], send, recv,
                device_id=(ix, peer), device_id_type=MESH,
            )
        )
    return copies


def arrived(ref, sem):
    pltpu.make_async_copy(ref, ref, sem).wait()


def ranks(onehot, onehot_b):
    before = (iota((CHUNK, CHUNK), 0) < iota((CHUNK, CHUNK), 1)).astype(F32).astype(BF16)
    ones = jnp.ones((CHUNK, CHUNK), BF16)
    carry = jnp.zeros((NDEV, CHUNK), F32)
    slots = []
    for c in range(ROWS // CHUNK):
        part = onehot_b[:, c * CHUNK : (c + 1) * CHUNK]
        rank = dot(part, before) + carry
        carry = carry + dot(part, ones)
        slots.append(jnp.sum(rank * onehot[:, c * CHUNK : (c + 1) * CHUNK], axis=0, keepdims=True))
    return slots


def hat(n, low, f):
    at = iota((n, CHUNK), 0)
    return jnp.where(at == low, 1.0 - f, jnp.where(at == low + 1, f, jnp.zeros_like(f)))


def stencils(base, frac, z_parts, w_xy):
    for c in range(ROWS // CHUNK):
        span = slice(c * CHUNK, (c + 1) * CHUNK)
        low = base[:, span]
        base_x = low // ((CZ - 1) * (CY - 1))
        rest = low - base_x * ((CZ - 1) * (CY - 1))
        base_y = rest // (CZ - 1)
        base_z = rest - base_y * (CZ - 1)
        fx, fy, fz = frac[0:1, span], frac[1:2, span], frac[2:3, span]
        hi, lo = two(hat(CZ, base_z, fz))
        z_parts[c, 0:CZ, :] = hi
        z_parts[c, CZ : 2 * CZ, :] = hi
        z_parts[c, 2 * CZ :, :] = lo
        w_x, w_y = hat(CX, base_x, fx), hat(CY, base_y, fy)
        for x in range(CX):
            w_xy[c, x] = w_x[x : x + 1] * w_y


def donate(c, hi, lo, z_parts, w_xy, slots, onehot_b, extra):
    top, rem = hi[...].reshape(CX * VY, CZ), lo[...].reshape(CX * VY, CZ)
    along = dot(jnp.concatenate([top, rem, top], axis=1), z_parts[c])
    at_slot = (iota((CAP, CHUNK), 0).astype(F32) == slots[c]).astype(F32)
    rows_hi, rows_lo = [], []
    for v in range(V):
        total = jnp.zeros((CY, CHUNK), F32)
        for x in range(CX):
            at = x * VY + v * CY
            total = total + along[at : at + CY] * w_xy[c, x]
        value = jnp.sum(total, axis=0, keepdims=True)
        first = value.astype(BF16).astype(F32)
        rows_hi.append((at_slot * first).astype(BF16))
        rows_lo.append((at_slot * (value - first)).astype(BF16))
    rows_hi += [(at_slot * part.astype(F32)).astype(BF16) for part in extra]
    return dot_t(jnp.concatenate(rows_hi + rows_lo, axis=0), onehot_b[:, c * CHUNK : (c + 1) * CHUNK])


def by_block(packed, extra):
    n, m = V * CAP, (V + extra) * CAP
    rows = [packed[:n] + packed[m:]] + ([packed[n:m]] if extra else []) + [jnp.zeros((128 - m, NDEV), F32)]
    return jnp.concatenate(rows, axis=0).T.reshape(GX, GY, 128)


def advance(count, flux_h, now_h, prev_h, jac_h, base_h, frac_h, dest_h, cell_h,
            later, hi_out, lo_out, halo2_x, halo2_y, km_xy, km_z,
            flux, q_now, q_prev, jac, base, frac, dest, cell, now_hi, now_lo, prev_hi, prev_lo, start, z_parts, w_xy,
            sent, mid, got, face_x, face_y, halo_x, halo_y, face2_x, face2_y, parts, places, at_z,
            load, send, recv, send2, recv2, send_a, recv_a, send_b, recv_b):
    loads = [
        pltpu.make_async_copy(a, b, load.at[i])
        for i, (a, b) in enumerate(
            [(dest_h, dest), (base_h, base), (frac_h, frac), (flux_h, flux), (cell_h, cell), (now_h, q_now),
             (jac_h, jac)]
        )
    ]
    for copy in loads[:5]:
        copy.start()
    for v in range(V):
        pltpu.make_async_copy(prev_h.at[v], q_prev.at[v], load.at[7]).start()
    ix, iy = lax.axis_index("gx"), lax.axis_index("gy")
    peers = [(lax.rem(ix + k, GX), iy) for k in range(1, GX)] + [(ix, lax.rem(iy + k, GY)) for k in range(1, GY)]
    barrier = pltpu.get_barrier_semaphore()
    for peer in peers:
        pl.semaphore_signal(barrier, inc=1, device_id=peer, device_id_type=MESH)

    def along_gx(wave):
        copies = []
        for k in range(1, GX):
            to = lax.rem(ix + k, GX)
            copies.append(
                pltpu.make_async_remote_copy(
                    sent.at[wave, to], mid.at[wave, ix], send_a.at[wave], recv_a.at[wave],
                    device_id=(to, iy), device_id_type=MESH,
                )
            )
        for copy in copies:
            copy.start()
        mid[wave, ix] = sent[wave, ix]

    def along_gy(wave):
        copies = []
        for k in range(1, GY):
            to = lax.rem(iy + k, GY)
            copies.append(
                pltpu.make_async_remote_copy(
                    mid.at[wave, :, to], got.at[wave, iy], send_b.at[wave], recv_b.at[wave],
                    device_id=(ix, to), device_id_type=MESH,
                )
            )
        for copy in copies:
            copy.start()
        got[wave, iy] = mid[wave, :, iy]

    for copy in loads[:5]:
        copy.wait()
    live = iota((1, ROWS), 1) < count[0]
    where_to = jnp.where(live, dest[...], NDEV)
    onehot = (iota((NDEV, ROWS), 0) == where_to).astype(F32)
    onehot_b = onehot.astype(BF16)
    slots = ranks(onehot, onehot_b)
    stencils(base, frac, z_parts, w_xy)
    mat_xy, mat_z = flux_matrix(flux)
    km_xy[...] = mat_xy
    km_z[...] = mat_z
    arrived(q_prev, load.at[7])
    for copy in loads[5:]:
        copy.start()
    for x in range(CX):
        for v in range(V):
            hi, lo = two(q_prev[v, x])
            prev_hi[x, v * CY : (v + 1) * CY, :] = hi
            prev_lo[x, v * CY : (v + 1) * CY, :] = lo
    packed = jnp.zeros((12 * CAP, NDEV), F32)
    for c in range(ROWS // CHUNK):
        cells = cell[:, c * CHUNK : (c + 1) * CHUNK]
        packed = packed + donate(
            c, prev_hi, prev_lo, z_parts, w_xy, slots, onehot_b, ((cells >> 8) + 1, cells & 255)
        )
    sent[0, :, :, 0, :] = by_block(packed, 2)

    pl.semaphore_wait(barrier, len(peers))
    along_gx(0)
    for copy in loads[5:]:
        copy.wait()
    for x in range(CX):
        for v in range(V):
            hi, lo = two(q_now[v, x])
            now_hi[x, v * CY : (v + 1) * CY, :] = hi
            now_lo[x, v * CY : (v + 1) * CY, :] = lo
    for v in range(V):
        for side, y in ((0, 0), (1, CY - 1)):
            for h in range(2):
                for p in range(2):
                    face_y[p, side, h, v * HALF : (v + 1) * HALF, :] = q_now[
                        v, p * HALF : (p + 1) * HALF, y, h * 128 : (h + 1) * 128
                    ]
        face_x[0, v * CY : (v + 1) * CY, :] = q_now[v, 0]
        face_x[1, v * CY : (v + 1) * CY, :] = q_now[v, CX - 1]
    for copy in x_copies(ix, iy, face_x, halo_x, send.at[0], recv.at[0]):
        copy.start()
    for p in range(2):
        for copy in y_copies(ix, iy, face_y, halo_y, p, send.at[1], recv.at[1]):
            copy.start()
    packed = jnp.zeros((10 * CAP, NDEV), F32)
    for c in range(ROWS // CHUNK):
        packed = packed + donate(c, now_hi, now_lo, z_parts, w_xy, slots, onehot_b, ())
    sent[1, :, :, 0, :] = by_block(packed, 0)
    along_gx(1)
    arrived(mid.at[0, pl.ds(0, GX - 1)], recv_a.at[0])
    along_gy(0)
    arrived(halo_x, recv.at[0])
    arrived(halo_y, recv.at[1])
    ends, rows = beyond(halo_x, halo_y)
    for x in range(CX):
        flux_x = flux_of(x, km_xy, km_z, now_hi, now_lo, ends, rows)
        scale = 0.2 * jac[x]
        for v in range(V):
            part = slice(v * CY, (v + 1) * CY)
            start[x, part, :] = q_now[v, x] - scale * (flux_x[part] + (q_prev[v, x] - q_now[v, x]))
    arrived(mid.at[1, pl.ds(0, GX - 1)], recv_a.at[1])
    along_gy(1)
    arrived(got.at[0, pl.ds(0, GY - 1)], recv_b.at[0])

    def spread(wave):
        rows = got[wave, :, :, 0, :].reshape(NDEV, 128)
        turned = rows.T
        for s in range(CAP):
            lanes = slice(s * NDEV, (s + 1) * NDEV)
            for v in range(V):
                hi, lo = two(jnp.broadcast_to(turned[v * CAP + s :][:1], (CY, NDEV)))
                parts[wave * 11 + v, :, lanes] = hi
                parts[wave * 11 + V + v, :, lanes] = lo
        return rows, turned

    rows, turned = spread(0)
    parts[10] = jnp.ones((CY, NDEV * CAP), BF16)
    for s in range(CAP):
        lanes = slice(s * NDEV, (s + 1) * NDEV)
        places[:, lanes] = jnp.broadcast_to(turned[5 * CAP + s :][:1], (CY, NDEV))
        column = rows[:, 6 * CAP + s : 6 * CAP + s + 1]
        at_z[lanes, :] = (iota((NDEV, CZ), 1).astype(F32) == column).astype(F32).astype(BF16)

    def landing(group, first, last):
        left = []
        for j in range(GROUP):
            mark = (iota((CY, 1), 0) + ((group * GROUP + j) * CY + 1)).astype(F32)
            here = (places[...] == mark).astype(F32).astype(BF16)
            left += [parts[i] * here for i in range(first, last)]
        return dot(jnp.concatenate(left, axis=0), at_z[...])

    def rows_of(landed, j, n, i):
        return landed[(j * n + i) * CY : (j * n + i + 1) * CY]

    for group in range(CX // GROUP):
        landed = landing(group, 0, 11)
        for j in range(GROUP):
            x = group * GROUP + j
            scale = 0.2 * jac[x]
            hits = rows_of(landed, j, 11, 10)
            for v in range(V):
                part = slice(v * CY, (v + 1) * CY)
                q, qp = q_now[v, x], q_prev[v, x]
                target = rows_of(landed, j, 11, v) + rows_of(landed, j, 11, V + v)
                w = start[x, part, :] - scale * (2.0 * (hits * q - target))
                hi, lo = two(w)
                hi_out[x, part, :] = hi
                lo_out[x, part, :] = lo
                later[x, part, :] = w - scale * ((3.0 * w - 4.0 * q + qp) + 2.0 * (hits * w))
                for side, y in ((0, 0), (1, CY - 1)):
                    for h in range(2):
                        row = w[y : y + 1, h * 128 : (h + 1) * 128]
                        at = v * HALF + x % HALF
                        face2_y[x // HALF, side, h, at : at + 1, :] = row
                if x in (0, CX - 1):
                    face2_x[0 if x == 0 else 1, part, :] = w
        if group % 2 == 1:
            p = group // 2
            for copy in y_copies(ix, iy, face2_y, halo2_y, p, send2.at[1 + p], recv2.at[1 + p]):
                copy.start()
    for copy in x_copies(ix, iy, face2_x, halo2_x, send2.at[0], recv2.at[0]):
        copy.start()
    arrived(got.at[1, pl.ds(0, GY - 1)], recv_b.at[1])
    spread(1)
    for group in range(CX // GROUP):
        landed = landing(group, 11, 21)
        for j in range(GROUP):
            x = group * GROUP + j
            scale = 0.4 * jac[x]
            for v in range(V):
                part = slice(v * CY, (v + 1) * CY)
                target = rows_of(landed, j, 10, v) + rows_of(landed, j, 10, V + v)
                later[x, part, :] = later[x, part, :] + scale * target
    for wave in range(2):
        arrived(sent.at[wave, pl.ds(0, GX - 1)], send_a.at[wave])
        arrived(got.at[wave, pl.ds(0, GY - 1)], send_b.at[wave])
    arrived(face_x, send.at[0])
    arrived(face_y, send.at[1])
    arrived(face2_x, send2.at[0])
    for p in range(2):
        arrived(face2_y.at[p], send2.at[1 + p])
        arrived(halo2_y.at[p], recv2.at[1 + p])
    arrived(halo2_x, recv2.at[0])


def second(hi, lo, later, jac, halo_x, halo_y, km_xy, km_z, out, plane, store):
    ends, rows = beyond(halo_x, halo_y)
    for x in range(CX):
        flux = flux_of(x, km_xy, km_z, hi, lo, ends, rows)
        scale = 0.2 * jac[x]
        for v in range(V):
            part = slice(v * CY, (v + 1) * CY)
            plane[x, v] = later[x, part, :] - scale * flux[part]
        pltpu.make_async_copy(plane.at[x], out.at[:, x], store.at[x]).start()
    for x in range(CX):
        pltpu.make_async_copy(plane.at[x], out.at[:, x], store.at[x]).wait()


VM = pl.BlockSpec(memory_space=pltpu.VMEM)
SM = pl.BlockSpec(memory_space=pltpu.SMEM)
HB = pl.BlockSpec(memory_space=pltpu.HBM)
FACES = [((2, VY, CZ), F32), ((2, 2, 2, V * HALF, 128), F32)]
PLANES = ((CX, VY, CZ), F32)
PARTS = [((CX, VY, CZ), BF16)] * 2
MATRIX = [((2 * VY, 256), BF16)] * 2


def shapes(entries):
    return [jax.ShapeDtypeStruct(*e) for e in entries]


def vmem(entries):
    return [pltpu.VMEM(*e) for e in entries]


def call_advance(count, flux, q_now, q_prev, jac, base, frac, dest, cell):
    ins = [pltpu.with_memory_space_constraint(a, pltpu.HBM) for a in (flux, q_now, q_prev, jac, base, frac, dest, cell)]
    dma = pltpu.SemaphoreType.DMA
    return pl.pallas_call(
        advance,
        out_shape=shapes([PLANES] + PARTS + FACES + MATRIX),
        in_specs=[SM] + [HB] * 8,
        out_specs=[VM] * 7,
        scratch_shapes=vmem([(a.shape, a.dtype) for a in ins])
        + vmem(PARTS * 2 + [PLANES, ((4, 3 * CZ, CHUNK), BF16), ((4, CX, CY, CHUNK), F32)])
        + vmem([((2, GX, GY, 1, 128), F32)] * 2 + [((2, GY, GX, 1, 128), F32)] + FACES * 3)
        + vmem([((21, CY, NDEV * CAP), BF16), ((CY, NDEV * CAP), F32), ((NDEV * CAP, CZ), BF16)])
        + [dma((8,))] + [dma((2,))] * 2 + [dma((3,))] * 2 + [dma((2,))] * 4,
        compiler_params=pltpu.CompilerParams(vmem_limit_bytes=LIMIT, collective_id=0, has_side_effects=True),
        name="advance",
    )(count, *ins)


def call_second(hi, lo, later, jac, halo_x, halo_y, km_xy, km_z):
    return pl.pallas_call(
        second,
        out_shape=jax.ShapeDtypeStruct((V, CX, CY, CZ), F32),
        in_specs=[VM] * 8,
        out_specs=HB,
        scratch_shapes=[pltpu.VMEM((CX, V, CY, CZ), F32), pltpu.SemaphoreType.DMA((CX,))],
        compiler_params=pltpu.CompilerParams(vmem_limit_bytes=LIMIT),
        name="second",
    )(hi, lo, later, jac, halo_x, halo_y, km_xy, km_z)


def body(q_now, q_prev, jacobian, flux_split, donor_base, donor_frac, fringe_dest, receptor_cell, fringe_count):
    later, hi, lo, halo_x, halo_y, km_xy, km_z = call_advance(
        fringe_count, flux_split.transpose(0, 2, 1, 3), q_now, q_prev, jacobian, donor_base.reshape(1, ROWS),
        donor_frac, fringe_dest.reshape(1, ROWS), receptor_cell.reshape(1, ROWS),
    )
    return call_second(hi, lo, later, jacobian, halo_x, halo_y, km_xy, km_z)


def solution(mesh):
    return jax.shard_map(
        body,
        mesh=mesh,
        in_specs=(
            P(None, "gx", "gy", None),
            P(None, "gx", "gy", None),
            P("gx", "gy", None),
            P(),
            P(("gx", "gy")),
            P(None, ("gx", "gy")),
            P(("gx", "gy"), None),
            P(("gx", "gy")),
            P(("gx", "gy")),
        ),
        out_specs=P(None, "gx", "gy", None),
        check_vma=False,
    )
```

```python
import jax
import jax.numpy as jnp
from jax import lax
from jax.experimental import pallas as pl
from jax.experimental.pallas import tpu as pltpu
from jax.sharding import PartitionSpec as P

MESH = pl.DeviceIdType.MESH
F32 = jnp.float32
BF16 = jnp.bfloat16
V, CX, CY, CZ = 5, 16, 16, 256
ROWS = 1024
NDEV = 128
CAP = 16
GX, GY = 8, 16
VY = V * CY
CHUNK = 256
GROUP = 8
HALF = CX // 2
LIMIT = 48 * 1024 * 1024


def iota(shape, dim):
    return lax.broadcasted_iota(jnp.int32, shape, dim)


def two(a):
    hi = a.astype(BF16)
    return hi, (a - hi.astype(F32)).astype(BF16)


def dot(a, b):
    return lax.dot_general(a, b, (((1,), (0,)), ((), ())), preferred_element_type=F32)


def dot_t(a, b):
    return lax.dot_general(a, b, (((1,), (1,)), ((), ())), preferred_element_type=F32)


def flux_matrix(flux):
    col = iota((1, 256), 1)
    block = (col >= 80).astype(jnp.int32) + (col >= 160).astype(jnp.int32) + (col >= 240).astype(jnp.int32)
    side = (col >= 248).astype(jnp.int32)
    var = jnp.where(block == 3, col - 240 - 8 * side, (col >> 4) - 5 * block)
    yc = jnp.where(block == 3, 17 * side - 1, col & 15)
    y = iota((CY, 256), 0)
    here = (yc == y).astype(F32)
    back = (yc == y - 1).astype(F32)
    fwd = (yc == y + 1).astype(F32)
    mid = (block == 1).astype(F32)
    near = ((block == 1) | (block == 3)).astype(F32)
    w_mid, w_back, w_fwd = here * mid, back * near, fwd * near
    w_any = here * (block < 3).astype(F32)
    w_left, w_right = here * (block == 0).astype(F32), here * (block == 2).astype(F32)
    mains, ups, downs = [], [], []
    for a in range(V):
        row = {}
        for d in range(3):
            for s in range(2):
                total = jnp.zeros((1, 256), F32)
                for b in range(V):
                    total = jnp.where(var == b, flux[d, a, s : s + 1, b : b + 1], total)
                row[d, s] = total
        centre = (row[0, 0] - row[0, 1]) + (row[1, 0] - row[1, 1]) + (row[2, 0] - row[2, 1])
        mains.append(
            centre * w_mid - row[1, 0] * w_back + row[1, 1] * w_fwd - row[0, 0] * w_left + row[0, 1] * w_right
        )
        ups.append(row[2, 1] * w_any)
        downs.append(row[2, 0] * w_any)
    hi, lo = two(jnp.concatenate(mains, axis=0))
    along = jnp.concatenate(ups + downs, axis=0)
    top = along.astype(BF16).astype(F32)
    return jnp.concatenate([hi, lo], axis=0), jnp.where(block == 1, along - top, top).astype(BF16)


def beyond(halo_x, halo_y):
    ix, iy = lax.axis_index("gx"), lax.axis_index("gy")
    nx, ny = lax.axis_size("gx"), lax.axis_size("gy")
    keep_x = [jnp.where(ix > 0, 1.0, 0.0), jnp.where(ix < nx - 1, 1.0, 0.0)]
    keep_y = [jnp.where(iy > 0, 1.0, 0.0), jnp.where(iy < ny - 1, 1.0, 0.0)]
    ends = [two(halo_x[side] * keep_x[side]) for side in range(2)]
    pad = jnp.zeros((8 - V, CZ), F32)

    def row(x):
        tiles = []
        for side in range(2):
            both = [halo_y[x // HALF, side, h, pl.ds(x % HALF, V, stride=HALF), :] for h in range(2)]
            tiles += [jnp.concatenate(both, axis=1) * keep_y[side], pad]
        return two(jnp.concatenate(tiles, axis=0))

    rows = [row(x) for x in range(CX)]
    return ends, rows


def flux_of(x, km_xy, km_z, hi, lo, ends, rows):
    def tile(ref, part):
        left = ends[0][part] if x == 0 else ref[x - 1]
        right = ends[1][part] if x == CX - 1 else ref[x + 1]
        return jnp.concatenate([left, ref[x], right, rows[x][part]], axis=0)

    both = dot(km_xy[...], tile(hi, 0))
    total = both[:VY] + both[VY:] + dot(km_xy[:VY], tile(lo, 1))
    along = dot(km_z[:, : 3 * VY], jnp.concatenate([hi[x], hi[x], lo[x]], axis=0))
    z = iota((VY, CZ), 1)
    fwd = jnp.where(z == CZ - 1, 0.0, pltpu.roll(along[:VY], CZ - 1, 1))
    back = jnp.where(z == 0, 0.0, pltpu.roll(along[VY:], 1, 1))
    return total + fwd - back


def x_copies(ix, iy, face_x, halo_x, send, recv):
    copies = []
    for side in range(2):
        peer = lax.rem(ix + 2 * side - 1 + GX, GX)
        copies.append(
            pltpu.make_async_remote_copy(
                face_x.at[side], halo_x.at[1 - side], send, recv, device_id=(peer, iy), device_id_type=MESH
            )
        )
    return copies


def y_copies(ix, iy, face_y, halo_y, piece, send, recv):
    copies = []
    for side in range(2):
        peer = lax.rem(iy + 2 * side - 1 + GY, GY)
        copies.append(
            pltpu.make_async_remote_copy(
                face_y.at[piece, side], halo_y.at[piece, 1 - side], send, recv,
                device_id=(ix, peer), device_id_type=MESH,
            )
        )
    return copies


def arrived(ref, sem):
    pltpu.make_async_copy(ref, ref, sem).wait()


def ranks(onehot, onehot_b):
    before = (iota((CHUNK, CHUNK), 0) < iota((CHUNK, CHUNK), 1)).astype(F32).astype(BF16)
    ones = jnp.ones((CHUNK, CHUNK), BF16)
    carry = jnp.zeros((NDEV, CHUNK), F32)
    slots = []
    for c in range(ROWS // CHUNK):
        part = onehot_b[:, c * CHUNK : (c + 1) * CHUNK]
        rank = dot(part, before) + carry
        carry = carry + dot(part, ones)
        slots.append(jnp.sum(rank * onehot[:, c * CHUNK : (c + 1) * CHUNK], axis=0, keepdims=True))
    return slots


def hat(n, low, f):
    at = iota((n, CHUNK), 0)
    return jnp.where(at == low, 1.0 - f, jnp.where(at == low + 1, f, jnp.zeros_like(f)))


def stencils(base, frac, z_parts, w_xy):
    for c in range(ROWS // CHUNK):
        span = slice(c * CHUNK, (c + 1) * CHUNK)
        low = base[:, span]
        base_x = low // ((CZ - 1) * (CY - 1))
        rest = low - base_x * ((CZ - 1) * (CY - 1))
        base_y = rest // (CZ - 1)
        base_z = rest - base_y * (CZ - 1)
        fx, fy, fz = frac[0:1, span], frac[1:2, span], frac[2:3, span]
        hi, lo = two(hat(CZ, base_z, fz))
        z_parts[c, 0:CZ, :] = hi
        z_parts[c, CZ : 2 * CZ, :] = hi
        z_parts[c, 2 * CZ :, :] = lo
        w_x, w_y = hat(CX, base_x, fx), hat(CY, base_y, fy)
        for x in range(CX):
            w_xy[c, x] = w_x[x : x + 1] * w_y


def donate(c, hi, lo, z_parts, w_xy, slots, onehot_b, extra):
    top, rem = hi[...].reshape(CX * VY, CZ), lo[...].reshape(CX * VY, CZ)
    along = dot(jnp.concatenate([top, rem, top], axis=1), z_parts[c])
    at_slot = (iota((CAP, CHUNK), 0).astype(F32) == slots[c]).astype(F32)
    rows_hi, rows_lo = [], []
    for v in range(V):
        total = jnp.zeros((CY, CHUNK), F32)
        for x in range(CX):
            at = x * VY + v * CY
            total = total + along[at : at + CY] * w_xy[c, x]
        value = jnp.sum(total, axis=0, keepdims=True)
        first = value.astype(BF16).astype(F32)
        rows_hi.append((at_slot * first).astype(BF16))
        rows_lo.append((at_slot * (value - first)).astype(BF16))
    rows_hi += [(at_slot * part.astype(F32)).astype(BF16) for part in extra]
    return dot_t(jnp.concatenate(rows_hi + rows_lo, axis=0), onehot_b[:, c * CHUNK : (c + 1) * CHUNK])


def by_block(packed, extra):
    n, m = V * CAP, (V + extra) * CAP
    rows = [packed[:n] + packed[m:]] + ([packed[n:m]] if extra else []) + [jnp.zeros((128 - m, NDEV), F32)]
    return jnp.concatenate(rows, axis=0).T.reshape(GX, GY, 128)


def advance(count, flux_h, now_h, prev_h, jac_h, base_h, frac_h, dest_h, cell_h,
            later, hi_out, lo_out, halo2_x, halo2_y, km_xy, km_z,
            flux, q_now, q_prev, jac, base, frac, dest, cell, now_hi, now_lo, prev_hi, prev_lo, start, z_parts, w_xy,
            sent, mid, got, face_x, face_y, halo_x, halo_y, face2_x, face2_y, parts, places, at_z,
            load, send, recv, send2, recv2, send_a, recv_a, send_b, recv_b):
    loads = [
        pltpu.make_async_copy(a, b, load.at[i])
        for i, (a, b) in enumerate(
            [(dest_h, dest), (base_h, base), (frac_h, frac), (flux_h, flux), (cell_h, cell), (now_h, q_now),
             (jac_h, jac)]
        )
    ]
    for copy in loads[:5]:
        copy.start()
    for v in range(V):
        pltpu.make_async_copy(prev_h.at[v], q_prev.at[v], load.at[7]).start()
    ix, iy = lax.axis_index("gx"), lax.axis_index("gy")
    peers = [(lax.rem(ix + k, GX), iy) for k in range(1, GX)] + [(ix, lax.rem(iy + k, GY)) for k in range(1, GY)]
    barrier = pltpu.get_barrier_semaphore()
    for peer in peers:
        pl.semaphore_signal(barrier, inc=1, device_id=peer, device_id_type=MESH)

    def along_gx(wave):
        copies = []
        for k in range(1, GX):
            to = lax.rem(ix + k, GX)
            copies.append(
                pltpu.make_async_remote_copy(
                    sent.at[wave, to], mid.at[wave, ix], send_a.at[wave], recv_a.at[wave],
                    device_id=(to, iy), device_id_type=MESH,
                )
            )
        for copy in copies:
            copy.start()
        mid[wave, ix] = sent[wave, ix]

    def along_gy(wave):
        copies = []
        for k in range(1, GY):
            to = lax.rem(iy + k, GY)
            copies.append(
                pltpu.make_async_remote_copy(
                    mid.at[wave, :, to], got.at[wave, iy], send_b.at[wave], recv_b.at[wave],
                    device_id=(ix, to), device_id_type=MESH,
                )
            )
        for copy in copies:
            copy.start()
        got[wave, iy] = mid[wave, :, iy]

    for copy in loads[:5]:
        copy.wait()
    live = iota((1, ROWS), 1) < count[0]
    where_to = jnp.where(live, dest[...], NDEV)
    onehot = (iota((NDEV, ROWS), 0) == where_to).astype(F32)
    onehot_b = onehot.astype(BF16)
    slots = ranks(onehot, onehot_b)
    stencils(base, frac, z_parts, w_xy)
    mat_xy, mat_z = flux_matrix(flux)
    km_xy[...] = mat_xy
    km_z[...] = mat_z
    arrived(q_prev, load.at[7])
    for copy in loads[5:]:
        copy.start()
    for x in range(CX):
        for v in range(V):
            hi, lo = two(q_prev[v, x])
            prev_hi[x, v * CY : (v + 1) * CY, :] = hi
            prev_lo[x, v * CY : (v + 1) * CY, :] = lo
    packed = jnp.zeros((12 * CAP, NDEV), F32)
    for c in range(ROWS // CHUNK):
        cells = cell[:, c * CHUNK : (c + 1) * CHUNK]
        packed = packed + donate(
            c, prev_hi, prev_lo, z_parts, w_xy, slots, onehot_b, ((cells >> 8) + 1, cells & 255)
        )
    sent[0, :, :, 0, :] = by_block(packed, 2)

    pl.semaphore_wait(barrier, len(peers))
    along_gx(0)
    for copy in loads[5:]:
        copy.wait()
    for x in range(CX):
        for v in range(V):
            hi, lo = two(q_now[v, x])
            now_hi[x, v * CY : (v + 1) * CY, :] = hi
            now_lo[x, v * CY : (v + 1) * CY, :] = lo
    for v in range(V):
        for side, y in ((0, 0), (1, CY - 1)):
            for h in range(2):
                for p in range(2):
                    face_y[p, side, h, v * HALF : (v + 1) * HALF, :] = q_now[
                        v, p * HALF : (p + 1) * HALF, y, h * 128 : (h + 1) * 128
                    ]
        face_x[0, v * CY : (v + 1) * CY, :] = q_now[v, 0]
        face_x[1, v * CY : (v + 1) * CY, :] = q_now[v, CX - 1]
    for copy in x_copies(ix, iy, face_x, halo_x, send.at[0], recv.at[0]):
        copy.start()
    for p in range(2):
        for copy in y_copies(ix, iy, face_y, halo_y, p, send.at[1], recv.at[1]):
            copy.start()
    packed = jnp.zeros((10 * CAP, NDEV), F32)
    for c in range(ROWS // CHUNK):
        packed = packed + donate(c, now_hi, now_lo, z_parts, w_xy, slots, onehot_b, ())
    sent[1, :, :, 0, :] = by_block(packed, 0)
    along_gx(1)
    arrived(mid.at[0, pl.ds(0, GX - 1)], recv_a.at[0])
    along_gy(0)
    arrived(halo_x, recv.at[0])
    arrived(halo_y, recv.at[1])
    ends, rows = beyond(halo_x, halo_y)
    for x in range(CX):
        flux_x = flux_of(x, km_xy, km_z, now_hi, now_lo, ends, rows)
        scale = 0.2 * jac[x]
        for v in range(V):
            part = slice(v * CY, (v + 1) * CY)
            start[x, part, :] = q_now[v, x] - scale * (flux_x[part] + (q_prev[v, x] - q_now[v, x]))
    arrived(mid.at[1, pl.ds(0, GX - 1)], recv_a.at[1])
    along_gy(1)
    arrived(got.at[0, pl.ds(0, GY - 1)], recv_b.at[0])

    def spread(wave):
        rows = got[wave, :, :, 0, :].reshape(NDEV, 128)
        turned = rows.T
        for s in range(CAP):
            lanes = slice(s * NDEV, (s + 1) * NDEV)
            for v in range(V):
                hi, lo = two(jnp.broadcast_to(turned[v * CAP + s :][:1], (CY, NDEV)))
                parts[wave * 11 + v, :, lanes] = hi
                parts[wave * 11 + V + v, :, lanes] = lo
        return rows, turned

    rows, turned = spread(0)
    parts[10] = jnp.ones((CY, NDEV * CAP), BF16)
    for s in range(CAP):
        lanes = slice(s * NDEV, (s + 1) * NDEV)
        places[:, lanes] = jnp.broadcast_to(turned[5 * CAP + s :][:1], (CY, NDEV))
        column = rows[:, 6 * CAP + s : 6 * CAP + s + 1]
        at_z[lanes, :] = (iota((NDEV, CZ), 1).astype(F32) == column).astype(F32).astype(BF16)

    def landing(group, first, last):
        left = []
        for j in range(GROUP):
            mark = (iota((CY, 1), 0) + ((group * GROUP + j) * CY + 1)).astype(F32)
            here = (places[...] == mark).astype(F32).astype(BF16)
            left += [parts[i] * here for i in range(first, last)]
        return dot(jnp.concatenate(left, axis=0), at_z[...])

    def rows_of(landed, j, n, i):
        return landed[(j * n + i) * CY : (j * n + i + 1) * CY]

    for group in range(CX // GROUP):
        landed = landing(group, 0, 11)
        for j in range(GROUP):
            x = group * GROUP + j
            scale = 0.2 * jac[x]
            hits = rows_of(landed, j, 11, 10)
            for v in range(V):
                part = slice(v * CY, (v + 1) * CY)
                q, qp = q_now[v, x], q_prev[v, x]
                target = rows_of(landed, j, 11, v) + rows_of(landed, j, 11, V + v)
                w = start[x, part, :] - scale * (2.0 * (hits * q - target))
                hi, lo = two(w)
                hi_out[x, part, :] = hi
                lo_out[x, part, :] = lo
                later[x, part, :] = w - scale * ((3.0 * w - 4.0 * q + qp) + 2.0 * (hits * w))
                for side, y in ((0, 0), (1, CY - 1)):
                    for h in range(2):
                        row = w[y : y + 1, h * 128 : (h + 1) * 128]
                        at = v * HALF + x % HALF
                        face2_y[x // HALF, side, h, at : at + 1, :] = row
                if x in (0, CX - 1):
                    face2_x[0 if x == 0 else 1, part, :] = w
    for p in range(2):
        for copy in y_copies(ix, iy, face2_y, halo2_y, p, send2.at[1 + p], recv2.at[1 + p]):
            copy.start()
    for copy in x_copies(ix, iy, face2_x, halo2_x, send2.at[0], recv2.at[0]):
        copy.start()
    arrived(got.at[1, pl.ds(0, GY - 1)], recv_b.at[1])
    spread(1)
    for group in range(CX // GROUP):
        landed = landing(group, 11, 21)
        for j in range(GROUP):
            x = group * GROUP + j
            scale = 0.4 * jac[x]
            for v in range(V):
                part = slice(v * CY, (v + 1) * CY)
                target = rows_of(landed, j, 10, v) + rows_of(landed, j, 10, V + v)
                later[x, part, :] = later[x, part, :] + scale * target
    for wave in range(2):
        arrived(sent.at[wave, pl.ds(0, GX - 1)], send_a.at[wave])
        arrived(got.at[wave, pl.ds(0, GY - 1)], send_b.at[wave])
    arrived(face_x, send.at[0])
    arrived(face_y, send.at[1])
    arrived(face2_x, send2.at[0])
    for p in range(2):
        arrived(face2_y.at[p], send2.at[1 + p])
        arrived(halo2_y.at[p], recv2.at[1 + p])
    arrived(halo2_x, recv2.at[0])


def second(hi, lo, later, jac, halo_x, halo_y, km_xy, km_z, out, plane, store):
    ends, rows = beyond(halo_x, halo_y)
    for x in range(CX):
        flux = flux_of(x, km_xy, km_z, hi, lo, ends, rows)
        scale = 0.2 * jac[x]
        for v in range(V):
            part = slice(v * CY, (v + 1) * CY)
            plane[x, v] = later[x, part, :] - scale * flux[part]
        pltpu.make_async_copy(plane.at[x], out.at[:, x], store.at[x]).start()
    for x in range(CX):
        pltpu.make_async_copy(plane.at[x], out.at[:, x], store.at[x]).wait()


VM = pl.BlockSpec(memory_space=pltpu.VMEM)
SM = pl.BlockSpec(memory_space=pltpu.SMEM)
HB = pl.BlockSpec(memory_space=pltpu.HBM)
FACES = [((2, VY, CZ), F32), ((2, 2, 2, V * HALF, 128), F32)]
PLANES = ((CX, VY, CZ), F32)
PARTS = [((CX, VY, CZ), BF16)] * 2
MATRIX = [((2 * VY, 256), BF16)] * 2


def shapes(entries):
    return [jax.ShapeDtypeStruct(*e) for e in entries]


def vmem(entries):
    return [pltpu.VMEM(*e) for e in entries]


def call_advance(count, flux, q_now, q_prev, jac, base, frac, dest, cell):
    ins = [pltpu.with_memory_space_constraint(a, pltpu.HBM) for a in (flux, q_now, q_prev, jac, base, frac, dest, cell)]
    dma = pltpu.SemaphoreType.DMA
    return pl.pallas_call(
        advance,
        out_shape=shapes([PLANES] + PARTS + FACES + MATRIX),
        in_specs=[SM] + [HB] * 8,
        out_specs=[VM] * 7,
        scratch_shapes=vmem([(a.shape, a.dtype) for a in ins])
        + vmem(PARTS * 2 + [PLANES, ((4, 3 * CZ, CHUNK), BF16), ((4, CX, CY, CHUNK), F32)])
        + vmem([((2, GX, GY, 1, 128), F32)] * 2 + [((2, GY, GX, 1, 128), F32)] + FACES * 3)
        + vmem([((21, CY, NDEV * CAP), BF16), ((CY, NDEV * CAP), F32), ((NDEV * CAP, CZ), BF16)])
        + [dma((8,))] + [dma((2,))] * 2 + [dma((3,))] * 2 + [dma((2,))] * 4,
        compiler_params=pltpu.CompilerParams(vmem_limit_bytes=LIMIT, collective_id=0, has_side_effects=True),
        name="advance",
    )(count, *ins)


def call_second(hi, lo, later, jac, halo_x, halo_y, km_xy, km_z):
    return pl.pallas_call(
        second,
        out_shape=jax.ShapeDtypeStruct((V, CX, CY, CZ), F32),
        in_specs=[VM] * 8,
        out_specs=HB,
        scratch_shapes=[pltpu.VMEM((CX, V, CY, CZ), F32), pltpu.SemaphoreType.DMA((CX,))],
        compiler_params=pltpu.CompilerParams(vmem_limit_bytes=LIMIT),
        name="second",
    )(hi, lo, later, jac, halo_x, halo_y, km_xy, km_z)


def body(q_now, q_prev, jacobian, flux_split, donor_base, donor_frac, fringe_dest, receptor_cell, fringe_count):
    later, hi, lo, halo_x, halo_y, km_xy, km_z = call_advance(
        fringe_count, flux_split.transpose(0, 2, 1, 3), q_now, q_prev, jacobian, donor_base.reshape(1, ROWS),
        donor_frac, fringe_dest.reshape(1, ROWS), receptor_cell.reshape(1, ROWS),
    )
    return call_second(hi, lo, later, jacobian, halo_x, halo_y, km_xy, km_z)


def solution(mesh):
    return jax.shard_map(
        body,
        mesh=mesh,
        in_specs=(
            P(None, "gx", "gy", None),
            P(None, "gx", "gy", None),
            P("gx", "gy", None),
            P(),
            P(("gx", "gy")),
            P(None, ("gx", "gy")),
            P(("gx", "gy"), None),
            P(("gx", "gy")),
            P(("gx", "gy")),
        ),
        out_specs=P(None, "gx", "gy", None),
        check_vma=False,
    )
```

```python
import jax
import jax.numpy as jnp
from jax import lax
from jax.experimental import pallas as pl
from jax.experimental.pallas import tpu as pltpu
from jax.sharding import PartitionSpec as P

MESH = pl.DeviceIdType.MESH
F32 = jnp.float32
BF16 = jnp.bfloat16
V, CX, CY, CZ = 5, 16, 16, 256
ROWS = 1024
NDEV = 128
CAP = 16
GX, GY = 8, 16
VY = V * CY
CHUNK = 256
GROUP = 8
HALF = CX // 2
LIMIT = 48 * 1024 * 1024


def iota(shape, dim):
    return lax.broadcasted_iota(jnp.int32, shape, dim)


def two(a):
    hi = a.astype(BF16)
    return hi, (a - hi.astype(F32)).astype(BF16)


def dot(a, b):
    return lax.dot_general(a, b, (((1,), (0,)), ((), ())), preferred_element_type=F32)


def dot_t(a, b):
    return lax.dot_general(a, b, (((1,), (1,)), ((), ())), preferred_element_type=F32)


def flux_matrix(flux):
    col = iota((1, 256), 1)
    block = (col >= 80).astype(jnp.int32) + (col >= 160).astype(jnp.int32) + (col >= 240).astype(jnp.int32)
    side = (col >= 248).astype(jnp.int32)
    var = jnp.where(block == 3, col - 240 - 8 * side, (col >> 4) - 5 * block)
    yc = jnp.where(block == 3, 17 * side - 1, col & 15)
    y = iota((CY, 256), 0)
    here = (yc == y).astype(F32)
    back = (yc == y - 1).astype(F32)
    fwd = (yc == y + 1).astype(F32)
    mid = (block == 1).astype(F32)
    near = ((block == 1) | (block == 3)).astype(F32)
    w_mid, w_back, w_fwd = here * mid, back * near, fwd * near
    w_any = here * (block < 3).astype(F32)
    w_left, w_right = here * (block == 0).astype(F32), here * (block == 2).astype(F32)
    mains, ups, downs = [], [], []
    for a in range(V):
        row = {}
        for d in range(3):
            for s in range(2):
                total = jnp.zeros((1, 256), F32)
                for b in range(V):
                    total = jnp.where(var == b, flux[d, a, s : s + 1, b : b + 1], total)
                row[d, s] = total
        centre = (row[0, 0] - row[0, 1]) + (row[1, 0] - row[1, 1]) + (row[2, 0] - row[2, 1])
        mains.append(
            centre * w_mid - row[1, 0] * w_back + row[1, 1] * w_fwd - row[0, 0] * w_left + row[0, 1] * w_right
        )
        ups.append(row[2, 1] * w_any)
        downs.append(row[2, 0] * w_any)
    hi, lo = two(jnp.concatenate(mains, axis=0))
    along = jnp.concatenate(ups + downs, axis=0)
    top = along.astype(BF16).astype(F32)
    return jnp.concatenate([hi, lo], axis=0), jnp.where(block == 1, along - top, top).astype(BF16)


def beyond(halo_x, halo_y):
    ix, iy = lax.axis_index("gx"), lax.axis_index("gy")
    nx, ny = lax.axis_size("gx"), lax.axis_size("gy")
    keep_x = [jnp.where(ix > 0, 1.0, 0.0), jnp.where(ix < nx - 1, 1.0, 0.0)]
    keep_y = [jnp.where(iy > 0, 1.0, 0.0), jnp.where(iy < ny - 1, 1.0, 0.0)]
    ends = [two(halo_x[side] * keep_x[side]) for side in range(2)]
    pad = jnp.zeros((8 - V, CZ), F32)

    def row(x):
        tiles = []
        for side in range(2):
            both = [halo_y[x // HALF, side, h, pl.ds(x % HALF, V, stride=HALF), :] for h in range(2)]
            tiles += [jnp.concatenate(both, axis=1) * keep_y[side], pad]
        return two(jnp.concatenate(tiles, axis=0))

    rows = [row(x) for x in range(CX)]
    return ends, rows


def flux_of(x, km_xy, km_z, hi, lo, ends, rows):
    def tile(ref, part):
        left = ends[0][part] if x == 0 else ref[x - 1]
        right = ends[1][part] if x == CX - 1 else ref[x + 1]
        return jnp.concatenate([left, ref[x], right, rows[x][part]], axis=0)

    both = dot(km_xy[...], tile(hi, 0))
    total = both[:VY] + both[VY:] + dot(km_xy[:VY], tile(lo, 1))
    along = dot(km_z[:, : 3 * VY], jnp.concatenate([hi[x], hi[x], lo[x]], axis=0))
    z = iota((VY, CZ), 1)
    fwd = jnp.where(z == CZ - 1, 0.0, pltpu.roll(along[:VY], CZ - 1, 1))
    back = jnp.where(z == 0, 0.0, pltpu.roll(along[VY:], 1, 1))
    return total + fwd - back


def x_copies(ix, iy, face_x, halo_x, send, recv):
    copies = []
    for side in range(2):
        peer = lax.rem(ix + 2 * side - 1 + GX, GX)
        copies.append(
            pltpu.make_async_remote_copy(
                face_x.at[side], halo_x.at[1 - side], send, recv, device_id=(peer, iy), device_id_type=MESH
            )
        )
    return copies


def y_copies(ix, iy, face_y, halo_y, piece, send, recv):
    copies = []
    for side in range(2):
        peer = lax.rem(iy + 2 * side - 1 + GY, GY)
        copies.append(
            pltpu.make_async_remote_copy(
                face_y.at[piece, side], halo_y.at[piece, 1 - side], send, recv,
                device_id=(ix, peer), device_id_type=MESH,
            )
        )
    return copies


def arrived(ref, sem):
    pltpu.make_async_copy(ref, ref, sem).wait()


def ranks(onehot, onehot_b):
    before = (iota((CHUNK, CHUNK), 0) < iota((CHUNK, CHUNK), 1)).astype(F32).astype(BF16)
    ones = jnp.ones((CHUNK, CHUNK), BF16)
    carry = jnp.zeros((NDEV, CHUNK), F32)
    slots = []
    for c in range(ROWS // CHUNK):
        part = onehot_b[:, c * CHUNK : (c + 1) * CHUNK]
        rank = dot(part, before) + carry
        carry = carry + dot(part, ones)
        slots.append(jnp.sum(rank * onehot[:, c * CHUNK : (c + 1) * CHUNK], axis=0, keepdims=True))
    return slots


def hat(n, low, f):
    at = iota((n, CHUNK), 0)
    return jnp.where(at == low, 1.0 - f, jnp.where(at == low + 1, f, jnp.zeros_like(f)))


def stencils(base, frac, z_parts, w_xy):
    for c in range(ROWS // CHUNK):
        span = slice(c * CHUNK, (c + 1) * CHUNK)
        low = base[:, span]
        base_x = low // ((CZ - 1) * (CY - 1))
        rest = low - base_x * ((CZ - 1) * (CY - 1))
        base_y = rest // (CZ - 1)
        base_z = rest - base_y * (CZ - 1)
        fx, fy, fz = frac[0:1, span], frac[1:2, span], frac[2:3, span]
        hi, lo = two(hat(CZ, base_z, fz))
        z_parts[c, 0:CZ, :] = hi
        z_parts[c, CZ : 2 * CZ, :] = hi
        z_parts[c, 2 * CZ :, :] = lo
        w_x, w_y = hat(CX, base_x, fx), hat(CY, base_y, fy)
        for x in range(CX):
            w_xy[c, x] = w_x[x : x + 1] * w_y


def donate(c, hi, lo, z_parts, w_xy, slots, onehot_b, extra):
    top, rem = hi[...].reshape(CX * VY, CZ), lo[...].reshape(CX * VY, CZ)
    along = dot(jnp.concatenate([top, rem, top], axis=1), z_parts[c])
    at_slot = (iota((CAP, CHUNK), 0).astype(F32) == slots[c]).astype(F32)
    rows_hi, rows_lo = [], []
    for v in range(V):
        total = jnp.zeros((CY, CHUNK), F32)
        for x in range(CX):
            at = x * VY + v * CY
            total = total + along[at : at + CY] * w_xy[c, x]
        value = jnp.sum(total, axis=0, keepdims=True)
        first = value.astype(BF16).astype(F32)
        rows_hi.append((at_slot * first).astype(BF16))
        rows_lo.append((at_slot * (value - first)).astype(BF16))
    rows_hi += [(at_slot * part.astype(F32)).astype(BF16) for part in extra]
    return dot_t(jnp.concatenate(rows_hi + rows_lo, axis=0), onehot_b[:, c * CHUNK : (c + 1) * CHUNK])


def by_block(packed, extra):
    n, m = V * CAP, (V + extra) * CAP
    rows = [packed[:n] + packed[m:]] + ([packed[n:m]] if extra else []) + [jnp.zeros((128 - m, NDEV), F32)]
    return jnp.concatenate(rows, axis=0).T.reshape(GX, GY, 128)


def advance(count, flux_h, now_h, prev_h, jac_h, base_h, frac_h, dest_h, cell_h,
            later, hi_out, lo_out, halo2_x, halo2_y, km_xy, km_z,
            flux, q_now, q_prev, jac, base, frac, dest, cell, now_hi, now_lo, prev_hi, prev_lo, start, z_parts, w_xy,
            sent, mid, got, face_x, face_y, halo_x, halo_y, face2_x, face2_y, parts, places, at_z,
            load, send, recv, send2, recv2, send_a, recv_a, send_b, recv_b):
    loads = [
        pltpu.make_async_copy(a, b, load.at[i])
        for i, (a, b) in enumerate(
            [(dest_h, dest), (base_h, base), (frac_h, frac), (flux_h, flux), (cell_h, cell), (now_h, q_now),
             (jac_h, jac)]
        )
    ]
    for copy in loads[:5]:
        copy.start()
    for v in range(V):
        pltpu.make_async_copy(prev_h.at[v], q_prev.at[v], load.at[7]).start()
    ix, iy = lax.axis_index("gx"), lax.axis_index("gy")
    peers = [(lax.rem(ix + k, GX), iy) for k in range(1, GX)] + [(ix, lax.rem(iy + k, GY)) for k in range(1, GY)]
    barrier = pltpu.get_barrier_semaphore()
    for peer in peers:
        pl.semaphore_signal(barrier, inc=1, device_id=peer, device_id_type=MESH)

    def along_gx(wave):
        copies = []
        for k in range(1, GX):
            to = lax.rem(ix + k, GX)
            copies.append(
                pltpu.make_async_remote_copy(
                    sent.at[wave, to], mid.at[wave, ix], send_a.at[wave], recv_a.at[wave],
                    device_id=(to, iy), device_id_type=MESH,
                )
            )
        for copy in copies:
            copy.start()
        mid[wave, ix] = sent[wave, ix]

    def along_gy(wave):
        copies = []
        for k in sorted(range(1, GY), key=lambda k: abs(k - GY // 2)):
            to = lax.rem(iy + k, GY)
            copies.append(
                pltpu.make_async_remote_copy(
                    mid.at[wave, :, to], got.at[wave, iy], send_b.at[wave], recv_b.at[wave],
                    device_id=(ix, to), device_id_type=MESH,
                )
            )
        for copy in copies:
            copy.start()
        got[wave, iy] = mid[wave, :, iy]

    for copy in loads[:5]:
        copy.wait()
    live = iota((1, ROWS), 1) < count[0]
    where_to = jnp.where(live, dest[...], NDEV)
    onehot = (iota((NDEV, ROWS), 0) == where_to).astype(F32)
    onehot_b = onehot.astype(BF16)
    slots = ranks(onehot, onehot_b)
    stencils(base, frac, z_parts, w_xy)
    mat_xy, mat_z = flux_matrix(flux)
    km_xy[...] = mat_xy
    km_z[...] = mat_z
    parts[10] = jnp.ones((CY, NDEV * CAP), BF16)
    arrived(q_prev, load.at[7])
    for copy in loads[5:]:
        copy.start()
    for x in range(CX):
        for v in range(V):
            hi, lo = two(q_prev[v, x])
            prev_hi[x, v * CY : (v + 1) * CY, :] = hi
            prev_lo[x, v * CY : (v + 1) * CY, :] = lo
    packed = jnp.zeros((12 * CAP, NDEV), F32)
    for c in range(ROWS // CHUNK):
        cells = cell[:, c * CHUNK : (c + 1) * CHUNK]
        packed = packed + donate(
            c, prev_hi, prev_lo, z_parts, w_xy, slots, onehot_b, ((cells >> 8) + 1, cells & 255)
        )
    sent[0, :, :, 0, :] = by_block(packed, 2)

    pl.semaphore_wait(barrier, len(peers))
    along_gx(0)
    for copy in loads[5:]:
        copy.wait()
    for x in range(CX):
        for v in range(V):
            hi, lo = two(q_now[v, x])
            now_hi[x, v * CY : (v + 1) * CY, :] = hi
            now_lo[x, v * CY : (v + 1) * CY, :] = lo
    for v in range(V):
        for side, y in ((0, 0), (1, CY - 1)):
            for h in range(2):
                for p in range(2):
                    face_y[p, side, h, v * HALF : (v + 1) * HALF, :] = q_now[
                        v, p * HALF : (p + 1) * HALF, y, h * 128 : (h + 1) * 128
                    ]
        face_x[0, v * CY : (v + 1) * CY, :] = q_now[v, 0]
        face_x[1, v * CY : (v + 1) * CY, :] = q_now[v, CX - 1]
    for copy in x_copies(ix, iy, face_x, halo_x, send.at[0], recv.at[0]):
        copy.start()
    for p in range(2):
        for copy in y_copies(ix, iy, face_y, halo_y, p, send.at[1], recv.at[1]):
            copy.start()
    packed = jnp.zeros((10 * CAP, NDEV), F32)
    for c in range(ROWS // CHUNK):
        packed = packed + donate(c, now_hi, now_lo, z_parts, w_xy, slots, onehot_b, ())
    sent[1, :, :, 0, :] = by_block(packed, 0)
    along_gx(1)
    arrived(mid.at[0, pl.ds(0, GX - 1)], recv_a.at[0])
    along_gy(0)
    arrived(halo_x, recv.at[0])
    arrived(halo_y, recv.at[1])
    ends, rows = beyond(halo_x, halo_y)
    for x in range(CX):
        flux_x = flux_of(x, km_xy, km_z, now_hi, now_lo, ends, rows)
        scale = 0.2 * jac[x]
        for v in range(V):
            part = slice(v * CY, (v + 1) * CY)
            start[x, part, :] = q_now[v, x] - scale * (flux_x[part] + (q_prev[v, x] - q_now[v, x]))
    arrived(mid.at[1, pl.ds(0, GX - 1)], recv_a.at[1])
    along_gy(1)
    arrived(got.at[0, pl.ds(0, GY - 1)], recv_b.at[0])

    def spread(wave):
        rows = got[wave, :, :, 0, :].reshape(NDEV, 128)
        turned = rows.T
        for s in range(CAP):
            lanes = slice(s * NDEV, (s + 1) * NDEV)
            for v in range(V):
                hi, lo = two(jnp.broadcast_to(turned[v * CAP + s :][:1], (CY, NDEV)))
                parts[wave * 11 + v, :, lanes] = hi
                parts[wave * 11 + V + v, :, lanes] = lo
        return rows, turned

    rows, turned = spread(0)
    for s in range(CAP):
        lanes = slice(s * NDEV, (s + 1) * NDEV)
        places[:, lanes] = jnp.broadcast_to(turned[5 * CAP + s :][:1], (CY, NDEV))
        column = rows[:, 6 * CAP + s : 6 * CAP + s + 1]
        at_z[lanes, :] = (iota((NDEV, CZ), 1).astype(F32) == column).astype(F32).astype(BF16)

    def landing(group, first, last):
        left = []
        for j in range(GROUP):
            mark = (iota((CY, 1), 0) + ((group * GROUP + j) * CY + 1)).astype(F32)
            here = (places[...] == mark).astype(F32).astype(BF16)
            left += [parts[i] * here for i in range(first, last)]
        return dot(jnp.concatenate(left, axis=0), at_z[...])

    def rows_of(landed, j, n, i):
        return landed[(j * n + i) * CY : (j * n + i + 1) * CY]

    for group in range(CX // GROUP):
        landed = landing(group, 0, 11)
        for j in range(GROUP):
            x = group * GROUP + j
            scale = 0.2 * jac[x]
            hits = rows_of(landed, j, 11, 10)
            for v in range(V):
                part = slice(v * CY, (v + 1) * CY)
                q, qp = q_now[v, x], q_prev[v, x]
                target = rows_of(landed, j, 11, v) + rows_of(landed, j, 11, V + v)
                w = start[x, part, :] - scale * (2.0 * (hits * q - target))
                hi, lo = two(w)
                hi_out[x, part, :] = hi
                lo_out[x, part, :] = lo
                later[x, part, :] = w - scale * ((3.0 * w - 4.0 * q + qp) + 2.0 * (hits * w))
                for side, y in ((0, 0), (1, CY - 1)):
                    for h in range(2):
                        row = w[y : y + 1, h * 128 : (h + 1) * 128]
                        at = v * HALF + x % HALF
                        face2_y[x // HALF, side, h, at : at + 1, :] = row
                if x in (0, CX - 1):
                    face2_x[0 if x == 0 else 1, part, :] = w
    for p in range(2):
        for copy in y_copies(ix, iy, face2_y, halo2_y, p, send2.at[1 + p], recv2.at[1 + p]):
            copy.start()
    for copy in x_copies(ix, iy, face2_x, halo2_x, send2.at[0], recv2.at[0]):
        copy.start()
    arrived(got.at[1, pl.ds(0, GY - 1)], recv_b.at[1])
    spread(1)
    for group in range(CX // GROUP):
        landed = landing(group, 11, 21)
        for j in range(GROUP):
            x = group * GROUP + j
            scale = 0.4 * jac[x]
            for v in range(V):
                part = slice(v * CY, (v + 1) * CY)
                target = rows_of(landed, j, 10, v) + rows_of(landed, j, 10, V + v)
                later[x, part, :] = later[x, part, :] + scale * target
    for wave in range(2):
        arrived(sent.at[wave, pl.ds(0, GX - 1)], send_a.at[wave])
        arrived(got.at[wave, pl.ds(0, GY - 1)], send_b.at[wave])
    arrived(face_x, send.at[0])
    arrived(face_y, send.at[1])
    arrived(face2_x, send2.at[0])
    for p in range(2):
        arrived(face2_y.at[p], send2.at[1 + p])
        arrived(halo2_y.at[p], recv2.at[1 + p])
    arrived(halo2_x, recv2.at[0])


def second(hi, lo, later, jac, halo_x, halo_y, km_xy, km_z, out, plane, store):
    ends, rows = beyond(halo_x, halo_y)
    for x in range(CX):
        flux = flux_of(x, km_xy, km_z, hi, lo, ends, rows)
        scale = 0.2 * jac[x]
        for v in range(V):
            part = slice(v * CY, (v + 1) * CY)
            plane[x, v] = later[x, part, :] - scale * flux[part]
        pltpu.make_async_copy(plane.at[x], out.at[:, x], store.at[x]).start()
    for x in range(CX):
        pltpu.make_async_copy(plane.at[x], out.at[:, x], store.at[x]).wait()


VM = pl.BlockSpec(memory_space=pltpu.VMEM)
SM = pl.BlockSpec(memory_space=pltpu.SMEM)
HB = pl.BlockSpec(memory_space=pltpu.HBM)
FACES = [((2, VY, CZ), F32), ((2, 2, 2, V * HALF, 128), F32)]
PLANES = ((CX, VY, CZ), F32)
PARTS = [((CX, VY, CZ), BF16)] * 2
MATRIX = [((2 * VY, 256), BF16)] * 2


def shapes(entries):
    return [jax.ShapeDtypeStruct(*e) for e in entries]


def vmem(entries):
    return [pltpu.VMEM(*e) for e in entries]


def call_advance(count, flux, q_now, q_prev, jac, base, frac, dest, cell):
    ins = [pltpu.with_memory_space_constraint(a, pltpu.HBM) for a in (flux, q_now, q_prev, jac, base, frac, dest, cell)]
    dma = pltpu.SemaphoreType.DMA
    return pl.pallas_call(
        advance,
        out_shape=shapes([PLANES] + PARTS + FACES + MATRIX),
        in_specs=[SM] + [HB] * 8,
        out_specs=[VM] * 7,
        scratch_shapes=vmem([(a.shape, a.dtype) for a in ins])
        + vmem(PARTS * 2 + [PLANES, ((4, 3 * CZ, CHUNK), BF16), ((4, CX, CY, CHUNK), F32)])
        + vmem([((2, GX, GY, 1, 128), F32)] * 2 + [((2, GY, GX, 1, 128), F32)] + FACES * 3)
        + vmem([((21, CY, NDEV * CAP), BF16), ((CY, NDEV * CAP), F32), ((NDEV * CAP, CZ), BF16)])
        + [dma((8,))] + [dma((2,))] * 2 + [dma((3,))] * 2 + [dma((2,))] * 4,
        compiler_params=pltpu.CompilerParams(vmem_limit_bytes=LIMIT, collective_id=0, has_side_effects=True),
        name="advance",
    )(count, *ins)


def call_second(hi, lo, later, jac, halo_x, halo_y, km_xy, km_z):
    return pl.pallas_call(
        second,
        out_shape=jax.ShapeDtypeStruct((V, CX, CY, CZ), F32),
        in_specs=[VM] * 8,
        out_specs=HB,
        scratch_shapes=[pltpu.VMEM((CX, V, CY, CZ), F32), pltpu.SemaphoreType.DMA((CX,))],
        compiler_params=pltpu.CompilerParams(vmem_limit_bytes=LIMIT),
        name="second",
    )(hi, lo, later, jac, halo_x, halo_y, km_xy, km_z)


def body(q_now, q_prev, jacobian, flux_split, donor_base, donor_frac, fringe_dest, receptor_cell, fringe_count):
    later, hi, lo, halo_x, halo_y, km_xy, km_z = call_advance(
        fringe_count, flux_split.transpose(0, 2, 1, 3), q_now, q_prev, jacobian, donor_base.reshape(1, ROWS),
        donor_frac, fringe_dest.reshape(1, ROWS), receptor_cell.reshape(1, ROWS),
    )
    return call_second(hi, lo, later, jacobian, halo_x, halo_y, km_xy, km_z)


def solution(mesh):
    return jax.shard_map(
        body,
        mesh=mesh,
        in_specs=(
            P(None, "gx", "gy", None),
            P(None, "gx", "gy", None),
            P("gx", "gy", None),
            P(),
            P(("gx", "gy")),
            P(None, ("gx", "gy")),
            P(("gx", "gy"), None),
            P(("gx", "gy")),
            P(("gx", "gy")),
        ),
        out_specs=P(None, "gx", "gy", None),
        check_vma=False,
    )
```
